256 devices in a mesh: row: 16 (over z, x_lo), col: 16 (over x_hi, y, core).
Axes of the slice: x: 4 (x_hi: 2, x_lo: 2; x = x_hi * 2 + x_lo), y: 4, z: 8, core: 2. Of those that a mesh axis runs over, the one named last changes fastest.
Arguments:
- src_points: bfloat16 [64, 16384], P(None, ('row', 'col')), may hold values from -24 to 24
- tgt_points: bfloat16 [64, 16384], P(None, ('col', 'row')), may hold values from -24 to 24
- grad_f: float32 [16384], P('row'), may hold values from -6 to 6
- grad_g: float32 [16384], P('col'), may hold values from -6 to 6
Outputs:
- grad_src: float32 [64, 16384], P(None, ('row', 'col'))
- grad_tgt: float32 [64, 16384], P(None, ('col', 'row'))
The draws below stay inside these ranges and needn't reach their ends.
All inputs are finite; a program needn't handle non-finite values.
Results may differ from the reference program's by a relative error of at most 0.0085.
Values may be sent and summed in bfloat16 or wider, within the bound.
A program may use at most 64 MiB of HBM per device.

```python
import math
import jax
import jax.numpy as jnp
from jax import lax

F = 64
PTS = 1024
SINK = 2
CG = 3
N = 16384
M = 16384


def scaled_points(key, count):
    base = jax.random.normal(key, (F, count), jnp.float32)
    return jnp.clip(base, -24.0, 24.0).astype(jnp.bfloat16)


def draw_src_points(key, part):
    return scaled_points(jax.random.fold_in(key, 101), N)


def draw_tgt_points(key, part):
    return scaled_points(jax.random.fold_in(key, 202), M)


def level_of(stream_key, extent, cuts, least, high):
    def one(dim, shards_of):
        steps = jax.random.uniform(jax.random.fold_in(jax.random.fold_in(stream_key, 6), dim), (shards_of,), jnp.float32, least / len(cuts), high / len(cuts))
        return jnp.repeat(jnp.exp(steps), extent[dim] // shards_of).reshape((-1,) + (1,) * (len(extent) - dim - 1))

    factor_of = one(*cuts[0])
    for cut in cuts[1:]:
        factor_of = factor_of * one(*cut)
    return factor_of


def gaussian(key, dims, scale, most, cuts=(), kind=jnp.bfloat16):
    drawn = scale * jax.random.normal(key, dims, jnp.float32)
    if cuts:
        drawn = drawn * level_of(key, dims, cuts, -0.22, 0.18)
    return jnp.clip(drawn, -most, most).astype(kind)


def setup_inputs(seed: int = 0) -> dict:
    seeds = jax.random.split(jax.random.key(seed), 5)
    return {
        "src_points": draw_src_points(jax.random.fold_in(seeds[4], 71), 0),
        "tgt_points": draw_tgt_points(jax.random.fold_in(seeds[4], 71), 0),
        "grad_f": gaussian(seeds[2], (N,), 1.0, 6.0, ((0, 16),), jnp.float32),
        "grad_g": gaussian(seeds[3], (M,), 1.0, 6.0, ((0, 16),), jnp.float32),
    }


EPS = 4.0
TAU = 0.1


def cost_tile(block_pts, block_sq, points_col, sq_col):
    cross = lax.dot_general(block_pts, points_col, (((0,), (0,)), ((), ())), preferred_element_type=jnp.float32)
    return block_sq[:, None] + sq_col[None, :] - 2.0 * cross


def reference(src_points, tgt_points, grad_f, grad_g):
    features, n_total = src_points.shape
    m_total = tgt_points.shape[1]
    block = min(512, PTS)
    block_count = n_total // block
    sq_row = jnp.sum(jnp.square(src_points.astype(jnp.float32)), axis=0)
    sq_col = jnp.sum(jnp.square(tgt_points.astype(jnp.float32)), axis=0)
    blocks_pts = jnp.moveaxis(src_points.reshape(features, block_count, block), 1, 0)
    blocks_sq = sq_row.reshape(block_count, block)
    shift = EPS * math.log(n_total / m_total)
    pot_col = jnp.zeros((m_total,), jnp.float32)
    pot_row = jnp.zeros((n_total,), jnp.float32)
    for iteration in range(SINK):
        def row_part(pieces):
            values = (pot_col[None, :] - cost_tile(pieces[0], pieces[1], tgt_points, sq_col)) / EPS
            highest = jnp.max(values, axis=1)
            return highest + jnp.log(jnp.sum(jnp.exp(values - highest[:, None]), axis=1))

        pot_row = -EPS * lax.map(row_part, (blocks_pts, blocks_sq)).reshape(-1)

        def col_part(carry, pieces):
            values = (pieces[2][:, None] - cost_tile(pieces[0], pieces[1], tgt_points, sq_col)) / EPS
            highest = jnp.maximum(carry[0], jnp.max(values, axis=0))
            totals = carry[1] * jnp.exp(carry[0] - highest) + jnp.sum(jnp.exp(values - highest[None, :]), axis=0)
            return (highest, totals), None

        start = (jnp.full((m_total,), -jnp.inf, jnp.float32), jnp.zeros((m_total,), jnp.float32))
        (highest, totals), unused = lax.scan(col_part, start, (blocks_pts, blocks_sq, pot_row.reshape(block_count, block)))
        pot_col = shift - EPS * (highest + jnp.log(totals))

    def plan_rows(pieces):
        cost = cost_tile(pieces[0], pieces[1], tgt_points, sq_col)
        return jnp.exp((pieces[2][:, None] + pot_col[None, :] - cost) / EPS).astype(jnp.bfloat16)

    plan_tile = lax.map(plan_rows, (blocks_pts, blocks_sq, pot_row.reshape(block_count, block))).reshape(n_total, m_total)
    row_mass = jnp.sum(plan_tile, axis=1, dtype=jnp.float32)
    col_mass = jnp.sum(plan_tile, axis=0, dtype=jnp.float32)

    def row_dot(vector):
        return jnp.sum(plan_tile * vector[None, :], axis=1)

    def col_dot(vector):
        return jnp.sum(plan_tile * vector[:, None], axis=0)

    def schur(vector):
        return (1.0 + TAU) * col_mass * vector - col_dot(row_dot(vector) / row_mass)

    rhs = grad_g - col_dot(grad_f / row_mass)
    dual_col = jnp.zeros_like(rhs)
    residual = rhs
    direction = rhs
    norm_now = jnp.sum(residual * residual)
    for iteration in range(CG):
        image = schur(direction)
        alpha = norm_now / jnp.sum(direction * image)
        dual_col = dual_col + alpha * direction
        residual = residual - alpha * image
        norm_next = jnp.sum(residual * residual)
        direction = residual + (norm_next / norm_now) * direction
        norm_now = norm_next
    dual_row = (grad_f - row_dot(dual_col)) / row_mass
    weights = (plan_tile * (dual_row[:, None] + dual_col[None, :])).astype(jnp.bfloat16)
    rows_w = jnp.sum(weights, axis=1, dtype=jnp.float32)
    cols_w = jnp.sum(weights, axis=0, dtype=jnp.float32)
    pulled_src = lax.dot_general(tgt_points, weights, (((1,), (1,)), ((), ())), preferred_element_type=jnp.float32)
    pulled_tgt = lax.dot_general(src_points, weights, (((1,), (0,)), ((), ())), preferred_element_type=jnp.float32)
    grad_src = 2.0 * (src_points.astype(jnp.float32) * rows_w[None, :] - pulled_src)
    grad_tgt = 2.0 * (tgt_points.astype(jnp.float32) * cols_w[None, :] - pulled_tgt)
    return grad_src, grad_tgt
```

```python
import functools

import jax
import jax.numpy as jnp
from jax import lax
from jax.experimental import pallas as pl
from jax.experimental.pallas import tpu as pltpu
from jax.sharding import PartitionSpec as P

CG = 3
TAU = 0.1
LANES = 128
MESH = pl.DeviceIdType.MESH
F32 = jnp.float32
BF16 = jnp.bfloat16

LR1, LC1, LR2, LC2, MASS, PULL, CMASS, A1 = range(8)
ROUNDS = 12


def ring(d, n):
    return min(d % n, n - d % n)


def kernel(
    sizes, src_ref, tgt_ref, gf_ref, gg_ref, osrc_ref, otgt_ref,
    pack_a, pack_b, gath_a, gath_b, gown_a, gown_b, gsl_a, gsl_b,
    x_ref, y_ref, c_ref, p_ref, fe_ref, lhs_ref, row_ref, acc_ref,
    mine, slots, emine, eslots, part_a, part_b, rs_a, rs_b,
    gsem, ssem, rsem, essem, ersem,
):
    nx, ny, nz, nc = sizes
    na, nb = nx * ny, nz * nc
    row, col = lax.axis_index("row"), lax.axis_index("col")
    z, x_lo = row // 2, row % 2
    x_hi, y, core = col // (2 * ny), (col // 2) % ny, col % 2
    x = x_hi * 2 + x_lo
    me_a, me_b = x * ny + y, z * nc + core
    feats, pts = src_ref.shape
    half = feats // 2
    ti, tj = na * pts, nb * pts
    ki, kj = ti // LANES, tj // LANES

    offs_a = [(i, j) for i in range(nx) for j in range(ny) if i or j]
    offs_a.sort(key=lambda o: -(ring(o[0], nx) + ring(o[1], ny)))
    offs_b = [(i, j) for i in range(nz) for j in range(nc) if i or j]
    offs_b.sort(key=lambda o: -(ring(o[0], nz) + 0.1 * o[1]))
    peers_a, peers_b = [], []
    for dx, dy in offs_a:
        px, py = (x + dx) % nx, (y + dy) % ny
        peers_a.append(((z * 2 + px % 2, (px // 2) * (2 * ny) + py * 2 + core), px * ny + py))
    for dz, dc in offs_b:
        pz, pc = (z + dz) % nz, (core + dc) % nc
        peers_b.append(((pz * 2 + x_lo, x_hi * (2 * ny) + y * 2 + pc), pz * nc + pc))

    def send(src, dst, s_sem, r_sem, dev):
        pltpu.make_async_remote_copy(
            src_ref=src, dst_ref=dst, send_sem=s_sem, recv_sem=r_sem, device_id=dev, device_id_type=MESH
        ).start()

    def wait_bytes(ref, sem):
        pltpu.make_async_copy(ref, ref, sem).wait()

    barrier = pltpu.get_barrier_semaphore()
    for dev, _ in peers_a + peers_b:
        pl.semaphore_signal(barrier, inc=1, device_id=dev, device_id_type=MESH)

    lane = lax.broadcasted_iota(jnp.int32, (half, LANES), 1)
    first = lane < pts
    lane1 = lax.broadcasted_iota(jnp.int32, (1, LANES), 1)
    first1 = lane1 < pts
    eye = lax.broadcasted_iota(jnp.int32, (LANES, LANES), 0) == lax.broadcasted_iota(
        jnp.int32, (LANES, LANES), 1
    )

    def pack(block):
        return jnp.concatenate([block[:half], block[half:]], axis=1).astype(BF16)

    pack_a[...] = pack(src_ref[...].astype(F32))
    pack_b[...] = pack(tgt_ref[...].astype(F32))

    def own(ref, at):
        line = ref[pl.ds(at // 2, 1), :]
        other = pltpu.roll(line, pts, 1)
        here = at % 2
        low = jnp.where(here == 0, line, other)
        high = jnp.where(here == 0, other, line)
        return jnp.where(first1, low, high)

    gown_a[...] = own(gf_ref, col)
    gown_b[...] = own(gg_ref, row)
    gath_a[me_a] = pack_a[...]
    gath_b[me_b] = pack_b[...]
    gsl_a[me_a] = gown_a[...]
    gsl_b[me_b] = gown_b[...]
    pl.semaphore_wait(barrier, na + nb - 2)

    for dev, _ in peers_b:
        send(pack_b, gath_b.at[me_b], gsem.at[0], gsem.at[1], dev)
    for dev, _ in peers_a:
        send(pack_a, gath_a.at[me_a], gsem.at[2], gsem.at[3], dev)
    for dev, _ in peers_b:
        send(gown_b, gsl_b.at[me_b], gsem.at[4], gsem.at[5], dev)
    for dev, _ in peers_a:
        send(gown_a, gsl_a.at[me_a], gsem.at[6], gsem.at[7], dev)

    def unpack(gath, out, k):
        one, two = gath[2 * k].astype(F32), gath[2 * k + 1].astype(F32)
        at = slice(k * LANES, (k + 1) * LANES)
        low = jnp.where(first, one, pltpu.roll(two, pts, 1))
        high = jnp.where(first, pltpu.roll(one, pts, 1), two)
        out[0:half, at] = low.astype(BF16)
        out[half:feats, at] = high.astype(BF16)
        return jnp.sum(low * low, axis=0, keepdims=True) + jnp.sum(high * high, axis=0, keepdims=True)

    pad = x_ref.shape[0] - feats
    tail_i = (lax.broadcasted_iota(jnp.int32, (pad, ti), 0) == 0).astype(F32).astype(BF16)
    tail_j = (lax.broadcasted_iota(jnp.int32, (pad, tj), 0) == 0).astype(F32).astype(BF16)
    x_ref[feats:, :] = tail_i
    y_ref[feats:, :] = tail_j

    wait_bytes(gath_a.at[pl.ds(0, na - 1)], gsem.at[3])
    sq_i = [unpack(gath_a, x_ref, k) for k in range(ki)]
    wait_bytes(gath_b.at[pl.ds(0, nb - 1)], gsem.at[1])
    sq_j = [unpack(gath_b, y_ref, k) for k in range(kj)]

    def upright(line):
        return jnp.sum(jnp.where(eye, line, 0.0), axis=1, keepdims=True)

    def flat(column):
        return jnp.sum(jnp.where(eye, column, 0.0), axis=0, keepdims=True)

    for k in range(ki):
        row_ref[k : k + 1, :] = sq_i[k]

    def row_lse(at, cols):
        top = None
        for s in range(kj):
            v = c_ref[s, at, :] if cols is None else c_ref[s, at, :] + cols[s]
            top = v if top is None else jnp.maximum(top, v)
        top = jnp.max(top, axis=1, keepdims=True)
        total = None
        for s in range(kj):
            v = c_ref[s, at, :] if cols is None else c_ref[s, at, :] + cols[s]
            e = jnp.exp(v - top)
            total = e if total is None else total + e
        total = jnp.sum(total, axis=1, keepdims=True)
        return top + jnp.log(total)

    def build(k, _):
        base = pl.multiple_of(k * LANES, LANES)
        at = pl.ds(base, LANES)
        cross = lax.dot_general(
            x_ref[0:feats, at], y_ref[0:feats, :], (((0,), (0,)), ((), ())), preferred_element_type=F32
        )
        up = upright(row_ref[pl.ds(k, 1), :])
        for s in range(kj):
            part = cross[:, s * LANES : (s + 1) * LANES]
            c_ref[s, at, :] = -0.25 * ((up + sq_j[s]) - 2.0 * part)
        mine[LR1, pl.ds(k, 1), :] = flat(row_lse(at, None))
        return 0

    lax.fori_loop(0, ki, build, 0)

    def post(i, peers):
        for s, (dev, _) in enumerate(peers):
            send(mine.at[i], slots.at[i, s], ssem.at[i], rsem.at[i], dev)

    def arrive(i, peers):
        n = len(peers)
        wait_bytes(slots.at[i, pl.ds(0, n)], rsem.at[i])
        return [mine[i]] + [slots[i, s] for s in range(n)]

    def tree(parts, op):
        while len(parts) > 1:
            parts = [op(parts[t], parts[t + 1]) if t + 1 < len(parts) else parts[t] for t in range(0, len(parts), 2)]
        return parts[0]

    def add(u, v):
        return u + v

    def lse_round(i, peers):
        post(i, peers)
        parts = arrive(i, peers)
        top = tree(parts, jnp.maximum)
        return -(top + jnp.log(tree([jnp.exp(p - top) for p in parts], add)))

    def sum_round(i, peers):
        post(i, peers)
        return tree(arrive(i, peers), add)

    def raise_rows(vector):
        row_ref[0:ki, :] = vector

        def one(k, _):
            at = pl.ds(pl.multiple_of(k * LANES, LANES), LANES)
            fe_ref[at, :] = jnp.broadcast_to(upright(row_ref[pl.ds(k, 1), :]), (LANES, LANES))
            return 0

        lax.fori_loop(0, ki, one, 0, unroll=2)

    def col_pass(i):
        def one(s, _):
            def highest(k, top):
                at = pl.ds(pl.multiple_of(k * LANES, LANES), LANES)
                v = c_ref[s, at, :] + fe_ref[at, :]
                return jnp.maximum(top, jnp.max(v.reshape(LANES // 8, 8, LANES), axis=0))

            top = lax.fori_loop(0, ki, highest, jnp.full((8, LANES), -jnp.inf, F32), unroll=2)
            top = jnp.max(top, axis=0, keepdims=True)

            def sums(k, total):
                at = pl.ds(pl.multiple_of(k * LANES, LANES), LANES)
                e = jnp.exp(c_ref[s, at, :] + fe_ref[at, :] - top)
                return total + jnp.sum(e.reshape(LANES // 8, 8, LANES), axis=0)

            total = lax.fori_loop(0, ki, sums, jnp.zeros((8, LANES), F32), unroll=2)
            total = jnp.sum(total, axis=0, keepdims=True)
            mine[i, pl.ds(s, 1), :] = top + jnp.log(total)
            return 0

        lax.fori_loop(0, kj, one, 0)

    def lines(vector):
        return [vector[s : s + 1, :] for s in range(vector.shape[0])]

    def row_pass(i, vector):
        cols = lines(vector)

        def one(k, _):
            at = pl.ds(pl.multiple_of(k * LANES, LANES), LANES)
            mine[i, pl.ds(k, 1), :] = flat(row_lse(at, cols))
            return 0

        lax.fori_loop(0, ki, one, 0)

    pot_row = lse_round(LR1, peers_a)
    raise_rows(pot_row)
    col_pass(LC1)
    pot_col = lse_round(LC1, peers_b)
    row_pass(LR2, pot_col)
    pot_row = lse_round(LR2, peers_a)
    raise_rows(pot_row)
    col_pass(LC2)
    pot_col = lse_round(LC2, peers_b)

    cols = lines(pot_col)

    def plan(k, _):
        at = pl.ds(pl.multiple_of(k * LANES, LANES), LANES)
        total = None
        for s in range(kj):
            e = jnp.exp((fe_ref[at, :] + cols[s]) + c_ref[s, at, :]).astype(BF16)
            p_ref[at, s * LANES : (s + 1) * LANES] = e
            e = e.astype(F32)
            total = e if total is None else total + e
        mine[MASS, pl.ds(k, 1), :] = flat(jnp.sum(total, axis=1, keepdims=True))
        return 0

    lax.fori_loop(0, ki, plan, 0)

    def load_lhs(vector, width):
        high = vector.astype(BF16).astype(F32)
        rest = vector - high
        mid = rest.astype(BF16).astype(F32)
        low = rest - mid
        for s in range(width // LANES):
            at = slice(s * LANES, (s + 1) * LANES)
            lhs_ref[0:1, at] = high[s : s + 1, :]
            lhs_ref[1:2, at] = mid[s : s + 1, :]
            lhs_ref[2:3, at] = low[s : s + 1, :]
        return lhs_ref[:, 0:width].astype(BF16)

    def row_dot(i, vector):
        got = lax.dot_general(
            load_lhs(vector, tj), p_ref[...], (((1,), (1,)), ((), ())), preferred_element_type=F32
        )
        got = got[0:1] + got[1:2] + got[2:3]
        for s in range(ki):
            mine[i, s : s + 1, :] = got[:, s * LANES : (s + 1) * LANES]

    def col_dot(i, vector, mass=None):
        got = jnp.dot(load_lhs(vector, ti), p_ref[...], preferred_element_type=F32)
        sums = got[0:1] + got[1:2] + got[2:3]
        for s in range(kj):
            at = slice(s * LANES, (s + 1) * LANES)
            mine[i, s : s + 1, :] = sums[:, at]
            if mass is not None:
                mine[mass, s : s + 1, :] = got[3:4, at]

    lhs_ref[...] = (lax.broadcasted_iota(jnp.int32, lhs_ref.shape, 0) == 3).astype(F32)
    row_mass = sum_round(MASS, peers_a)

    wait_bytes(gsl_a.at[pl.ds(0, na - 1)], gsem.at[7])
    wait_bytes(gsl_b.at[pl.ds(0, nb - 1)], gsem.at[5])
    for k in range(ki):
        row_ref[k : k + 1, :] = jnp.where(first1, gsl_a[2 * k], gsl_a[2 * k + 1])
    grad_f = row_ref[0:ki, :]
    for k in range(kj):
        row_ref[k : k + 1, :] = jnp.where(first1, gsl_b[2 * k], gsl_b[2 * k + 1])
    grad_g = row_ref[0:kj, :]

    col_dot(PULL, grad_f / row_mass, CMASS)
    post(CMASS, peers_b)
    post(PULL, peers_b)
    col_mass = tree(arrive(CMASS, peers_b), add)
    residual = grad_g - tree(arrive(PULL, peers_b), add)

    def line_sum(v):
        return jnp.sum(v, axis=0, keepdims=True)

    def extra_post(i, peers):
        for s, (dev, _) in enumerate(peers):
            send(emine.at[i], eslots.at[i, s], essem.at[i], ersem.at[i], dev)

    def extra_arrive(i, peers):
        n = len(peers)
        wait_bytes(eslots.at[i, pl.ds(0, n)], ersem.at[i])
        got = tree([emine[i]] + [eslots[i, s] for s in range(n)], add)
        return jnp.sum(got, axis=1, keepdims=True)

    emine[...] = jnp.zeros_like(emine)
    dual = pulled_dual = direction = applied = norm = d_c_d = None
    for it in range(CG):
        i_a, i_b = A1 + 2 * it, A1 + 2 * it + 1
        e_a, e_b = 2 * it, 2 * it + 1
        weighted = col_mass * residual
        emine[e_a, 0:1, :] = line_sum(residual * residual)
        emine[e_a, 1:2, :] = line_sum(weighted * residual)
        if it:
            emine[e_a, 2:3, :] = line_sum(weighted * direction)
        extra_post(e_a, peers_a)
        row_dot(i_a, residual)
        post(i_a, peers_a)
        scal = extra_arrive(e_a, peers_a)
        fresh = tree(arrive(i_a, peers_a), add)
        if it:
            beta = scal[0:1] / norm
            direction = residual + beta * direction
            applied = fresh + beta * applied
            d_c_d = scal[1:2] + 2.0 * beta * scal[2:3] + beta * beta * d_c_d
        else:
            direction, applied, d_c_d = residual, fresh, scal[1:2]
        norm = scal[0:1]
        back = applied / row_mass
        emine[e_b, 0:1, :] = line_sum(applied * back)
        extra_post(e_b, peers_b)
        if it < CG - 1:
            col_dot(i_b, back)
            post(i_b, peers_b)
        q_q = extra_arrive(e_b, peers_b)[0:1]
        alpha = norm / ((1.0 + TAU) * d_c_d - q_q)
        dual = alpha * direction if dual is None else dual + alpha * direction
        pulled_dual = alpha * applied if pulled_dual is None else pulled_dual + alpha * applied
        if it < CG - 1:
            image = (1.0 + TAU) * col_mass * direction - tree(arrive(i_b, peers_b), add)
            residual = residual - alpha * image

    dual_row = (grad_f - pulled_dual) / row_mass
    raise_rows(dual_row)
    cols_w = lines(dual)

    acc_ref[...] = jnp.zeros_like(acc_ref)

    def weigh(k, _):
        at = pl.ds(pl.multiple_of(k * LANES, LANES), LANES)
        up = fe_ref[at, :]
        w = jnp.concatenate(
            [
                (p_ref[at, s * LANES : (s + 1) * LANES].astype(F32) * (up + cols_w[s])).astype(BF16)
                for s in range(kj)
            ],
            axis=1,
        )
        acc_ref[...] += jnp.dot(x_ref[:, at], w, preferred_element_type=F32)
        pulled = lax.dot_general(y_ref[...], w, (((1,), (1,)), ((), ())), preferred_element_type=F32)
        spread(x_ref[0:feats, at], pulled, part_a, k)
        return 0

    def spread(points, pulled, part, k):
        grad = 2.0 * (points.astype(F32) * pulled[feats : feats + 1, :] - pulled[0:feats, :])
        low, high = grad[0:half], grad[half:feats]
        part[2 * k] = jnp.where(first, low, pltpu.roll(high, pts, 1)).astype(BF16)
        part[2 * k + 1] = jnp.where(first, pltpu.roll(low, pts, 1), high).astype(BF16)

    lax.fori_loop(0, ki, weigh, 0)
    for k in range(kj):
        at = slice(k * LANES, (k + 1) * LANES)
        spread(y_ref[0:feats, at], acc_ref[:, at], part_b, k)
    for s, (dev, peer) in enumerate(peers_b):
        send(part_b.at[peer], rs_b.at[s], gsem.at[8], gsem.at[9], dev)
    for s, (dev, peer) in enumerate(peers_a):
        send(part_a.at[peer], rs_a.at[s], gsem.at[10], gsem.at[11], dev)

    def collect(part, me, slot, n, sem, out):
        wait_bytes(slot, sem)
        got = tree([part[me].astype(F32)] + [slot[s].astype(F32) for s in range(n)], add)
        out[0:half, :] = got[:, 0:pts]
        out[half:feats, :] = got[:, pts:]

    collect(part_a, me_a, rs_a, na - 1, gsem.at[11], osrc_ref)
    collect(part_b, me_b, rs_b, nb - 1, gsem.at[9], otgt_ref)

    wait_bytes(gath_b.at[pl.ds(0, nb - 1)], gsem.at[0])
    wait_bytes(gath_a.at[pl.ds(0, na - 1)], gsem.at[2])
    wait_bytes(gsl_b.at[pl.ds(0, nb - 1)], gsem.at[4])
    wait_bytes(gsl_a.at[pl.ds(0, na - 1)], gsem.at[6])
    wait_bytes(rs_b, gsem.at[8])
    wait_bytes(rs_a, gsem.at[10])
    group = {i: peers_a for i in (LR1, LR2, MASS, A1, A1 + 2, A1 + 4)}
    for i in range(ROUNDS):
        wait_bytes(slots.at[i, pl.ds(0, len(group.get(i, peers_b)))], ssem.at[i])
    for e in range(2 * CG):
        wait_bytes(eslots.at[e, pl.ds(0, len(peers_a if e % 2 == 0 else peers_b))], essem.at[e])


def body(sizes, src_points, tgt_points, grad_f, grad_g):
    nx, ny, nz, nc = sizes
    feats, pts = src_points.shape
    na, nb = nx * ny, nz * nc
    ti, tj = na * pts, nb * pts
    ki, kj = ti // LANES, tj // LANES
    n = max(na, nb) - 1
    k = max(ki, kj)
    half = feats // 2
    vmem = pl.BlockSpec(memory_space=pltpu.VMEM)
    out = jax.ShapeDtypeStruct((feats, pts), F32)
    return pl.pallas_call(
        functools.partial(kernel, sizes),
        out_shape=(out, out),
        in_specs=[vmem] * 4,
        out_specs=(vmem, vmem),
        scratch_shapes=[
            pltpu.VMEM((half, LANES), BF16),
            pltpu.VMEM((half, LANES), BF16),
            pltpu.VMEM((na, half, LANES), BF16),
            pltpu.VMEM((nb, half, LANES), BF16),
            pltpu.VMEM((1, LANES), F32),
            pltpu.VMEM((1, LANES), F32),
            pltpu.VMEM((na, 1, LANES), F32),
            pltpu.VMEM((nb, 1, LANES), F32),
            pltpu.VMEM((feats + 16, ti), BF16),
            pltpu.VMEM((feats + 16, tj), BF16),
            pltpu.VMEM((kj, ti, LANES), F32),
            pltpu.VMEM((ti, tj), BF16),
            pltpu.VMEM((ti, LANES), F32),
            pltpu.VMEM((8, max(ti, tj)), F32),
            pltpu.VMEM((k, LANES), F32),
            pltpu.VMEM((feats + 16, tj), F32),
            pltpu.VMEM((ROUNDS, k, LANES), F32),
            pltpu.VMEM((ROUNDS, n, k, LANES), F32),
            pltpu.VMEM((2 * CG, 4, LANES), F32),
            pltpu.VMEM((2 * CG, n, 4, LANES), F32),
            pltpu.VMEM((na, half, LANES), BF16),
            pltpu.VMEM((nb, half, LANES), BF16),
            pltpu.VMEM((na - 1, half, LANES), BF16),
            pltpu.VMEM((nb - 1, half, LANES), BF16),
            pltpu.SemaphoreType.DMA((12,)),
            pltpu.SemaphoreType.DMA((ROUNDS,)),
            pltpu.SemaphoreType.DMA((ROUNDS,)),
            pltpu.SemaphoreType.DMA((2 * CG,)),
            pltpu.SemaphoreType.DMA((2 * CG,)),
        ],
        compiler_params=pltpu.CompilerParams(
            collective_id=0, has_side_effects=True, vmem_limit_bytes=40 * 1024 * 1024
        ),
        name="transport",
    )(src_points, tgt_points, grad_f.reshape(-1, LANES), grad_g.reshape(-1, LANES))


def solution(mesh):
    rows, cols = mesh.shape["row"], mesh.shape["col"]
    sizes = (4, cols // 4, rows // 2, 2)
    in_specs = (P(None, ("row", "col")), P(None, ("col", "row")), P("row"), P("col"))
    out_specs = (P(None, ("row", "col")), P(None, ("col", "row")))
    return jax.shard_map(
        functools.partial(body, sizes), mesh=mesh, in_specs=in_specs, out_specs=out_specs, check_vma=False
    )
```

```python
import functools
import math

import jax
import jax.numpy as jnp
from jax import lax
from jax.experimental import pallas as pl
from jax.experimental.pallas import tpu as pltpu
from jax.sharding import PartitionSpec as P

CG = 3
TAU = 0.1
LOG2E = math.log2(math.e)
LANES = 128
MESH = pl.DeviceIdType.MESH
F32 = jnp.float32
BF16 = jnp.bfloat16

LR1, LC1, LR2, LC2, MASS, PULL, CMASS, A1 = range(8)
ROUNDS = 12


def ring(d, n):
    return min(d % n, n - d % n)


def kernel(
    sizes, src_hbm, tgt_hbm, gf_hbm, gg_hbm, osrc_ref, otgt_ref,
    src_ref, tgt_ref, gf_ref, gg_ref,
    pack_a, pack_b, gath_a, gath_b, gown_a, gown_b, gsl_a, gsl_b,
    x_ref, y_ref, c_ref, ct_ref, p_ref, fe_ref, lhs_ref, row_ref, xu_ref, yw_ref, xp_ref, yp_ref,
    mine, slots, emine, eslots, part_a, part_b, rs_a, rs_b,
    isem, gsem, ssem, rsem, essem, ersem, sga, rga, sgb, rgb,
):
    nx, ny, nz, nc = sizes
    na, nb = nx * ny, nz * nc
    row, col = lax.axis_index("row"), lax.axis_index("col")
    z, x_lo = row // 2, row % 2
    x_hi, y, core = col // (2 * ny), (col // 2) % ny, col % 2
    x = x_hi * 2 + x_lo
    me_a, me_b = x * ny + y, z * nc + core
    feats, pts = src_ref.shape
    half = feats // 2
    ti, tj = na * pts, nb * pts
    ki, kj = ti // LANES, tj // LANES

    offs_a = [(i, j) for i in range(nx) for j in range(ny) if i or j]
    offs_a.sort(key=lambda o: -(ring(o[0], nx) + ring(o[1], ny)))
    offs_b = [(i, j) for i in range(nz) for j in range(nc) if i or j]
    offs_b.sort(key=lambda o: -(ring(o[0], nz) + 0.1 * o[1]))
    peers_a, peers_b = [], []
    for dx, dy in offs_a:
        px, py = (x + dx) % nx, (y + dy) % ny
        peers_a.append(((z * 2 + px % 2, (px // 2) * (2 * ny) + py * 2 + core), px * ny + py))
    for dz, dc in offs_b:
        pz, pc = (z + dz) % nz, (core + dc) % nc
        peers_b.append(((pz * 2 + x_lo, x_hi * (2 * ny) + y * 2 + pc), pz * nc + pc))

    def send(src, dst, s_sem, r_sem, dev):
        pltpu.make_async_remote_copy(
            src_ref=src, dst_ref=dst, send_sem=s_sem, recv_sem=r_sem, device_id=dev, device_id_type=MESH
        ).start()

    def wait_bytes(ref, sem):
        pltpu.make_async_copy(ref, ref, sem).wait()

    barrier = pltpu.get_barrier_semaphore()
    for dev, _ in peers_a + peers_b:
        pl.semaphore_signal(barrier, inc=1, device_id=dev, device_id_type=MESH)
    loads = [
        pltpu.make_async_copy(here, there, isem.at[n])
        for n, (here, there) in enumerate(
            ((src_hbm, src_ref), (tgt_hbm, tgt_ref), (gf_hbm, gf_ref), (gg_hbm, gg_ref))
        )
    ]
    for load in loads:
        load.start()

    first = lax.broadcasted_iota(jnp.int32, (half, LANES), 1) < pts
    first1 = lax.broadcasted_iota(jnp.int32, (1, LANES), 1) < pts
    lhs_ref[...] = jnp.zeros_like(lhs_ref)
    emine[...] = jnp.zeros_like(emine)
    for ref in (x_ref, y_ref):
        pad = (ref.shape[0] - feats, ref.shape[1])
        ref[feats:, :] = (lax.broadcasted_iota(jnp.int32, pad, 0) == 0).astype(F32).astype(BF16)

    def pack(block):
        return jnp.concatenate([block[:half], block[half:]], axis=1).astype(BF16)

    def own(ref, at):
        line = ref[pl.ds(at // 2, 1), :]
        other = pltpu.roll(line, pts, 1)
        here = at % 2
        low = jnp.where(here == 0, line, other)
        high = jnp.where(here == 0, other, line)
        return jnp.where(first1, low, high)

    for load in loads:
        load.wait()
    pack_a[...] = pack(src_ref[...].astype(F32))
    pack_b[...] = pack(tgt_ref[...].astype(F32))
    gown_a[...] = own(gf_ref, col)
    gown_b[...] = own(gg_ref, row)
    gath_a[me_a] = pack_a[...]
    gath_b[me_b] = pack_b[...]
    gsl_a[me_a] = gown_a[...]
    gsl_b[me_b] = gown_b[...]
    pl.semaphore_wait(barrier, na + nb - 2)

    for dev, _ in peers_b:
        send(pack_b, gath_b.at[me_b], gsem.at[0], gsem.at[1], dev)
    for dev, _ in peers_a:
        send(pack_a, gath_a.at[me_a], gsem.at[2], gsem.at[3], dev)
    for dev, _ in peers_b:
        send(gown_b, gsl_b.at[me_b], gsem.at[4], gsem.at[5], dev)
    for dev, _ in peers_a:
        send(gown_a, gsl_a.at[me_a], gsem.at[6], gsem.at[7], dev)

    def unpack(gath, out, k):
        one, two = gath[2 * k].astype(F32), gath[2 * k + 1].astype(F32)
        at = slice(k * LANES, (k + 1) * LANES)
        low = jnp.where(first, one, pltpu.roll(two, pts, 1))
        high = jnp.where(first, pltpu.roll(one, pts, 1), two)
        out[0:half, at] = low.astype(BF16)
        out[half:feats, at] = high.astype(BF16)
        return 0.25 * jnp.sum(low * low + high * high, axis=0, keepdims=True)

    wait_bytes(gath_a.at[pl.ds(0, na - 1)], gsem.at[3])
    sq_i = [unpack(gath_a, x_ref, k) for k in range(ki)]
    wait_bytes(gath_b.at[pl.ds(0, nb - 1)], gsem.at[1])
    sq_j = [unpack(gath_b, y_ref, k) for k in range(kj)]

    def upright(line):
        return jnp.broadcast_to(line, (LANES, LANES)).T

    def lanes(k):
        return slice(k * LANES, (k + 1) * LANES)

    def build(out, tall, sq_tall, wide, sq_wide):
        for k, line in enumerate(sq_tall):
            cross = lax.dot_general(
                tall[0:feats, lanes(k)], wide[0:feats, :], (((0,), (0,)), ((), ())), preferred_element_type=F32
            )
            up = upright(line)
            for s, other in enumerate(sq_wide):
                out[s, lanes(k), :] = LOG2E * (0.5 * cross[:, lanes(s)] - (up + other))

    STEP = 16

    def lse_pass(i, tile, vector):
        chunks, height = tile.shape[0], tile.shape[1]
        cols = None if vector is None else lines(vector)
        for k in range(height // LANES):
            tops, sums = [], []
            for h in range(k * LANES, (k + 1) * LANES, STEP):
                vs = [tile[s, h : h + STEP, :] for s in range(chunks)]
                if cols is not None:
                    vs = [v + c for v, c in zip(vs, cols)]
                top = tree(vs, jnp.maximum)
                tops.append(top)
                sums.append(tree([jnp.exp2(v - top) for v in vs], add))
            top = jnp.concatenate(tops, axis=0).T
            total = jnp.concatenate(sums, axis=0).T
            best = jnp.max(top, axis=0, keepdims=True)
            total = jnp.sum(total * jnp.exp2(top - best), axis=0, keepdims=True)
            mine[i, k : k + 1, :] = best + jnp.log2(total)

    def post(i, peers):
        for s, (dev, _) in enumerate(peers):
            send(mine.at[i], slots.at[i, s], ssem.at[i], rsem.at[i], dev)

    def arrive(i, peers):
        n = len(peers)
        wait_bytes(slots.at[i, pl.ds(0, n)], rsem.at[i])
        return [mine[i]] + [slots[i, s] for s in range(n)]

    def tree(parts, op):
        while len(parts) > 1:
            parts = [op(parts[t], parts[t + 1]) if t + 1 < len(parts) else parts[t] for t in range(0, len(parts), 2)]
        return parts[0]

    def add(u, v):
        return u + v

    def lse_end(i, peers):
        parts = arrive(i, peers)
        top = tree(parts, jnp.maximum)
        return -(top + jnp.log2(tree([jnp.exp2(p - top) for p in parts], add)))

    def lines(vector):
        return [vector[s : s + 1, :] for s in range(vector.shape[0])]

    build(c_ref, x_ref, sq_i, y_ref, sq_j)
    lse_pass(LR1, c_ref, None)
    post(LR1, peers_a)
    build(ct_ref, y_ref, sq_j, x_ref, sq_i)
    pot_row = lse_end(LR1, peers_a)
    lse_pass(LC1, ct_ref, pot_row)
    post(LC1, peers_b)
    pot_col = lse_end(LC1, peers_b)
    lse_pass(LR2, c_ref, pot_col)
    post(LR2, peers_a)
    pot_row = lse_end(LR2, peers_a)
    lse_pass(LC2, ct_ref, pot_row)
    post(LC2, peers_b)
    for k, line in enumerate(lines(pot_row)):
        fe_ref[lanes(k), :] = upright(line)
    pot_col = lse_end(LC2, peers_b)

    cols = lines(pot_col)
    for k in range(ki):
        totals = []
        for h in range(k * LANES, (k + 1) * LANES, STEP):
            up = fe_ref[h : h + STEP, :]
            parts = []
            for s in range(kj):
                e = jnp.exp2((up + cols[s]) + c_ref[s, h : h + STEP, :]).astype(BF16)
                p_ref[h : h + STEP, lanes(s)] = e
                parts.append(e.astype(F32))
            totals.append(tree(parts, add))
        mine[MASS, k : k + 1, :] = jnp.sum(jnp.concatenate(totals, axis=0).T, axis=0, keepdims=True)
    post(MASS, peers_a)

    def wide_dot(left):
        return jnp.dot(left, p_ref[...], preferred_element_type=F32)

    def tall_dot(left):
        return lax.dot_general(left, p_ref[...], (((1,), (1,)), ((), ())), preferred_element_type=F32)

    xp_ref[...] = wide_dot(x_ref[...])
    for s in range(kj):
        mine[CMASS, s : s + 1, :] = xp_ref[feats : feats + 1, lanes(s)]
    post(CMASS, peers_b)
    yp_ref[...] = tall_dot(y_ref[...])
    wait_bytes(gsl_a.at[pl.ds(0, na - 1)], gsem.at[7])
    wait_bytes(gsl_b.at[pl.ds(0, nb - 1)], gsem.at[5])
    for k in range(ki):
        row_ref[k : k + 1, :] = jnp.where(first1, gsl_a[2 * k], gsl_a[2 * k + 1])
    grad_f = row_ref[0:ki, :]
    for k in range(kj):
        row_ref[k : k + 1, :] = jnp.where(first1, gsl_b[2 * k], gsl_b[2 * k + 1])
    grad_g = row_ref[0:kj, :]

    def load_lhs(vector, width):
        high = vector.astype(BF16).astype(F32)
        rest = vector - high
        mid = rest.astype(BF16).astype(F32)
        low = rest - mid
        for s in range(width // LANES):
            lhs_ref[0:1, lanes(s)] = high[s : s + 1, :]
            lhs_ref[1:2, lanes(s)] = mid[s : s + 1, :]
            lhs_ref[2:3, lanes(s)] = low[s : s + 1, :]
        return lhs_ref[:, 0:width].astype(BF16)

    def keep(i, got):
        got = got[0:1] + got[1:2] + got[2:3]
        for s in range(got.shape[1] // LANES):
            mine[i, s : s + 1, :] = got[:, lanes(s)]

    def row_dot(i, vector):
        keep(i, tall_dot(load_lhs(vector, tj)))
        post(i, peers_a)

    def col_dot(i, vector):
        keep(i, wide_dot(load_lhs(vector, ti)))
        post(i, peers_b)

    row_mass = tree(arrive(MASS, peers_a), add)
    col_dot(PULL, grad_f / row_mass)
    col_mass = tree(arrive(CMASS, peers_b), add)
    residual = grad_g - tree(arrive(PULL, peers_b), add)

    def line_sum(v):
        return jnp.sum(v, axis=0, keepdims=True)

    def extra_post(i, peers):
        for s, (dev, _) in enumerate(peers):
            send(emine.at[i], eslots.at[i, s], essem.at[i], ersem.at[i], dev)

    def extra_arrive(i, peers):
        n = len(peers)
        wait_bytes(eslots.at[i, pl.ds(0, n)], ersem.at[i])
        got = tree([emine[i]] + [eslots[i, s] for s in range(n)], add)
        return jnp.sum(got, axis=1, keepdims=True)

    def spread(points, pulled, part, k):
        grad = 2.0 * (points.astype(F32) * pulled[feats : feats + 1, :] - pulled[0:feats, :])
        low, high = grad[0:half], grad[half:feats]
        part[2 * k] = jnp.where(first, low, pltpu.roll(high, pts, 1)).astype(BF16)
        part[2 * k + 1] = jnp.where(first, pltpu.roll(low, pts, 1), high).astype(BF16)

    def split(out, points, factors):
        rows = points.shape[0]
        for s, factor in enumerate(factors):
            v = points[:, lanes(s)].astype(F32) * factor
            high = v.astype(BF16)
            out[0:rows, lanes(s)] = high
            out[rows : 2 * rows, lanes(s)] = (v - high.astype(F32)).astype(BF16)

    rows = feats + 16

    def gradients(g, on_row, on_col):
        us, ws = lines(on_row), lines(on_col)
        split(yw_ref, y_ref, ws)
        got = tall_dot(yw_ref[...])
        split(xu_ref, x_ref, us)
        for k in range(ki):
            pulled = got[0:rows, lanes(k)] + got[rows:, lanes(k)] + us[k] * yp_ref[:, lanes(k)]
            spread(x_ref[0:feats, lanes(k)], pulled, part_a.at[g], k)
        for s, (dev, peer) in enumerate(peers_a):
            send(part_a.at[g, peer], rs_a.at[g, s], sga.at[g], rga.at[g], dev)
        got = wide_dot(xu_ref[...])
        for k in range(kj):
            pulled = got[0:rows, lanes(k)] + got[rows:, lanes(k)] + ws[k] * xp_ref[:, lanes(k)]
            spread(y_ref[0:feats, lanes(k)], pulled, part_b.at[g], k)
        for s, (dev, peer) in enumerate(peers_b):
            send(part_b.at[g, peer], rs_b.at[g, s], sgb.at[g], rgb.at[g], dev)

    dual = pulled_dual = direction = applied = norm = d_c_d = None
    for it in range(CG):
        i_a, i_b = A1 + 2 * it, A1 + 2 * it + 1
        e_a, e_b = 2 * it, 2 * it + 1
        weighted = col_mass * residual
        emine[e_a, 0:1, :] = line_sum(residual * residual)
        emine[e_a, 1:2, :] = line_sum(weighted * residual)
        if it:
            emine[e_a, 2:3, :] = line_sum(weighted * direction)
        extra_post(e_a, peers_a)
        row_dot(i_a, residual)
        if it == CG - 1:
            gradients(0, (grad_f - pulled_dual) / row_mass, dual)
        scal = extra_arrive(e_a, peers_a)
        fresh = tree(arrive(i_a, peers_a), add)
        if it:
            beta = scal[0:1] / norm
            direction = residual + beta * direction
            applied = fresh + beta * applied
            d_c_d = scal[1:2] + 2.0 * beta * scal[2:3] + beta * beta * d_c_d
        else:
            direction, applied, d_c_d = residual, fresh, scal[1:2]
        norm = scal[0:1]
        back = applied / row_mass
        emine[e_b, 0:1, :] = line_sum(applied * back)
        extra_post(e_b, peers_b)
        if it == CG - 1:
            gradients(1, -back, direction)
            q_q = extra_arrive(e_b, peers_b)[0:1]
            alpha = norm / ((1.0 + TAU) * d_c_d - q_q)
            continue
        col_dot(i_b, back)
        q_q = extra_arrive(e_b, peers_b)[0:1]
        alpha = norm / ((1.0 + TAU) * d_c_d - q_q)
        dual = alpha * direction if it == 0 else dual + alpha * direction
        pulled_dual = alpha * applied if it == 0 else pulled_dual + alpha * applied
        image = (1.0 + TAU) * col_mass * direction - tree(arrive(i_b, peers_b), add)
        residual = residual - alpha * image

    def collect(g, part, me, slot, n, sem):
        wait_bytes(slot.at[g], sem.at[g])
        return tree([part[g, me].astype(F32)] + [slot[g, s].astype(F32) for s in range(n)], add)

    def store(out, got):
        out[0:half, :] = got[:, 0:pts]
        out[half:feats, :] = got[:, pts:]

    base_a = collect(0, part_a, me_a, rs_a, na - 1, rga)
    base_b = collect(0, part_b, me_b, rs_b, nb - 1, rgb)
    store(osrc_ref, base_a + alpha * collect(1, part_a, me_a, rs_a, na - 1, rga))
    store(otgt_ref, base_b + alpha * collect(1, part_b, me_b, rs_b, nb - 1, rgb))

    wait_bytes(gath_b.at[pl.ds(0, nb - 1)], gsem.at[0])
    wait_bytes(gath_a.at[pl.ds(0, na - 1)], gsem.at[2])
    wait_bytes(gsl_b.at[pl.ds(0, nb - 1)], gsem.at[4])
    wait_bytes(gsl_a.at[pl.ds(0, na - 1)], gsem.at[6])
    for g in range(2):
        wait_bytes(rs_a.at[g], sga.at[g])
        wait_bytes(rs_b.at[g], sgb.at[g])
    over_a = (LR1, LR2, MASS, A1, A1 + 2, A1 + 4)
    for i in range(ROUNDS):
        wait_bytes(slots.at[i, pl.ds(0, len(peers_a if i in over_a else peers_b))], ssem.at[i])
    for e in range(2 * CG):
        wait_bytes(eslots.at[e, pl.ds(0, len(peers_a if e % 2 == 0 else peers_b))], essem.at[e])


def body(sizes, src_points, tgt_points, grad_f, grad_g):
    nx, ny, nz, nc = sizes
    feats, pts = src_points.shape
    na, nb = nx * ny, nz * nc
    ti, tj = na * pts, nb * pts
    ki, kj = ti // LANES, tj // LANES
    n = max(na, nb) - 1
    k = max(ki, kj)
    half = feats // 2
    rows = feats + 16
    vmem = pl.BlockSpec(memory_space=pltpu.VMEM)
    out = jax.ShapeDtypeStruct((feats, pts), F32)
    return pl.pallas_call(
        functools.partial(kernel, sizes),
        out_shape=(out, out),
        in_specs=[pl.BlockSpec(memory_space=pl.ANY)] * 4,
        out_specs=(vmem, vmem),
        scratch_shapes=[
            pltpu.VMEM((feats, pts), BF16),
            pltpu.VMEM((feats, pts), BF16),
            pltpu.VMEM((grad_f.shape[0] // LANES, LANES), F32),
            pltpu.VMEM((grad_g.shape[0] // LANES, LANES), F32),
            pltpu.VMEM((half, LANES), BF16),
            pltpu.VMEM((half, LANES), BF16),
            pltpu.VMEM((na, half, LANES), BF16),
            pltpu.VMEM((nb, half, LANES), BF16),
            pltpu.VMEM((1, LANES), F32),
            pltpu.VMEM((1, LANES), F32),
            pltpu.VMEM((na, 1, LANES), F32),
            pltpu.VMEM((nb, 1, LANES), F32),
            pltpu.VMEM((rows, ti), BF16),
            pltpu.VMEM((rows, tj), BF16),
            pltpu.VMEM((kj, ti, LANES), F32),
            pltpu.VMEM((ki, tj, LANES), F32),
            pltpu.VMEM((ti, tj), BF16),
            pltpu.VMEM((ti, LANES), F32),
            pltpu.VMEM((8, max(ti, tj)), F32),
            pltpu.VMEM((k, LANES), F32),
            pltpu.VMEM((2 * rows, ti), BF16),
            pltpu.VMEM((2 * rows, tj), BF16),
            pltpu.VMEM((rows, tj), F32),
            pltpu.VMEM((rows, ti), F32),
            pltpu.VMEM((ROUNDS, k, LANES), F32),
            pltpu.VMEM((ROUNDS, n, k, LANES), F32),
            pltpu.VMEM((2 * CG, 4, LANES), F32),
            pltpu.VMEM((2 * CG, n, 4, LANES), F32),
            pltpu.VMEM((2, na, half, LANES), BF16),
            pltpu.VMEM((2, nb, half, LANES), BF16),
            pltpu.VMEM((2, na - 1, half, LANES), BF16),
            pltpu.VMEM((2, nb - 1, half, LANES), BF16),
            pltpu.SemaphoreType.DMA((4,)),
            pltpu.SemaphoreType.DMA((8,)),
            pltpu.SemaphoreType.DMA((ROUNDS,)),
            pltpu.SemaphoreType.DMA((ROUNDS,)),
            pltpu.SemaphoreType.DMA((2 * CG,)),
            pltpu.SemaphoreType.DMA((2 * CG,)),
            pltpu.SemaphoreType.DMA((2,)),
            pltpu.SemaphoreType.DMA((2,)),
            pltpu.SemaphoreType.DMA((2,)),
            pltpu.SemaphoreType.DMA((2,)),
        ],
        compiler_params=pltpu.CompilerParams(
            collective_id=0, has_side_effects=True, vmem_limit_bytes=40 * 1024 * 1024
        ),
        name="transport",
    )(src_points, tgt_points, grad_f.reshape(-1, LANES), grad_g.reshape(-1, LANES))


def solution(mesh):
    rows, cols = mesh.shape["row"], mesh.shape["col"]
    sizes = (4, cols // 4, rows // 2, 2)
    in_specs = (P(None, ("row", "col")), P(None, ("col", "row")), P("row"), P("col"))
    out_specs = (P(None, ("row", "col")), P(None, ("col", "row")))
    return jax.shard_map(
        functools.partial(body, sizes), mesh=mesh, in_specs=in_specs, out_specs=out_specs, check_vma=False
    )
```

```python
import functools
import math

import jax
import jax.numpy as jnp
from jax import lax
from jax.experimental import pallas as pl
from jax.experimental.pallas import tpu as pltpu
from jax.sharding import PartitionSpec as P

CG = 3
TAU = 0.1
LOG2E = math.log2(math.e)
LANES = 128
MESH = pl.DeviceIdType.MESH
F32 = jnp.float32
BF16 = jnp.bfloat16

LR1, LC1, LR2, LC2, MASS, PULL, CMASS, A1 = range(8)
ROUNDS = 12


def ring(d, n):
    return min(d % n, n - d % n)


def kernel(
    sizes, src_hbm, tgt_hbm, gf_hbm, gg_hbm, osrc_ref, otgt_ref,
    src_ref, tgt_ref, gf_ref, gg_ref,
    pack_a, pack_b, gath_a, gath_b, gown_a, gown_b, gsl_a, gsl_b,
    x_ref, y_ref, c_ref, ct_ref, p_ref, fe_ref, lhs_ref, row_ref, xu_ref, yw_ref, xp_ref, yp_ref, yk_ref,
    mine, slots, emine, eslots, part_a, part_b, rs_a, rs_b,
    isem, gsem, ssem, rsem, essem, ersem, sga, rga, sgb, rgb,
):
    nx, ny, nz, nc = sizes
    na, nb = nx * ny, nz * nc
    row, col = lax.axis_index("row"), lax.axis_index("col")
    z, x_lo = row // 2, row % 2
    x_hi, y, core = col // (2 * ny), (col // 2) % ny, col % 2
    x = x_hi * 2 + x_lo
    me_a, me_b = x * ny + y, z * nc + core
    feats, pts = src_ref.shape
    half = feats // 2
    ti, tj = na * pts, nb * pts
    ki, kj = ti // LANES, tj // LANES

    offs_a = [(i, j) for i in range(nx) for j in range(ny) if i or j]
    offs_a.sort(key=lambda o: -(ring(o[0], nx) + ring(o[1], ny)))
    offs_b = [(i, j) for i in range(nz) for j in range(nc) if i or j]
    offs_b.sort(key=lambda o: -(ring(o[0], nz) + 0.1 * o[1]))
    peers_a, peers_b = [], []
    for dx, dy in offs_a:
        px, py = (x + dx) % nx, (y + dy) % ny
        peers_a.append(((z * 2 + px % 2, (px // 2) * (2 * ny) + py * 2 + core), px * ny + py))
    for dz, dc in offs_b:
        pz, pc = (z + dz) % nz, (core + dc) % nc
        peers_b.append(((pz * 2 + x_lo, x_hi * (2 * ny) + y * 2 + pc), pz * nc + pc))

    def send(src, dst, s_sem, r_sem, dev):
        pltpu.make_async_remote_copy(
            src_ref=src, dst_ref=dst, send_sem=s_sem, recv_sem=r_sem, device_id=dev, device_id_type=MESH
        ).start()

    def wait_bytes(ref, sem):
        pltpu.make_async_copy(ref, ref, sem).wait()

    barrier = pltpu.get_barrier_semaphore()
    for dev, _ in peers_a + peers_b:
        pl.semaphore_signal(barrier, inc=1, device_id=dev, device_id_type=MESH)
    loads = [
        pltpu.make_async_copy(here, there, isem.at[n])
        for n, (here, there) in enumerate(
            ((src_hbm, src_ref), (tgt_hbm, tgt_ref), (gf_hbm, gf_ref), (gg_hbm, gg_ref))
        )
    ]
    for load in loads:
        load.start()

    first = lax.broadcasted_iota(jnp.int32, (half, LANES), 1) < pts
    first1 = lax.broadcasted_iota(jnp.int32, (1, LANES), 1) < pts
    lhs_ref[...] = jnp.zeros_like(lhs_ref)
    emine[...] = jnp.zeros_like(emine)
    for ref in (x_ref, y_ref):
        pad = (ref.shape[0] - feats, ref.shape[1])
        ref[feats:, :] = (lax.broadcasted_iota(jnp.int32, pad, 0) == 0).astype(F32).astype(BF16)

    def pack(block):
        return jnp.concatenate([block[:half], block[half:]], axis=1).astype(BF16)

    def own(ref, at):
        line = ref[pl.ds(at // 2, 1), :]
        other = pltpu.roll(line, pts, 1)
        here = at % 2
        low = jnp.where(here == 0, line, other)
        high = jnp.where(here == 0, other, line)
        return jnp.where(first1, low, high)

    for load in loads:
        load.wait()
    pack_a[...] = pack(src_ref[...].astype(F32))
    pack_b[...] = pack(tgt_ref[...].astype(F32))
    gown_a[...] = own(gf_ref, col)
    gown_b[...] = own(gg_ref, row)
    gath_a[me_a] = pack_a[...]
    gath_b[me_b] = pack_b[...]
    gsl_a[me_a] = gown_a[...]
    gsl_b[me_b] = gown_b[...]
    pl.semaphore_wait(barrier, na + nb - 2)

    for dev, _ in peers_b:
        send(pack_b, gath_b.at[me_b], gsem.at[0], gsem.at[1], dev)
    for dev, _ in peers_a:
        send(pack_a, gath_a.at[me_a], gsem.at[2], gsem.at[3], dev)
    for dev, _ in peers_b:
        send(gown_b, gsl_b.at[me_b], gsem.at[4], gsem.at[5], dev)
    for dev, _ in peers_a:
        send(gown_a, gsl_a.at[me_a], gsem.at[6], gsem.at[7], dev)

    def unpack(gath, out, k):
        one, two = gath[2 * k].astype(F32), gath[2 * k + 1].astype(F32)
        at = slice(k * LANES, (k + 1) * LANES)
        low = jnp.where(first, one, pltpu.roll(two, pts, 1))
        high = jnp.where(first, pltpu.roll(one, pts, 1), two)
        out[0:half, at] = low.astype(BF16)
        out[half:feats, at] = high.astype(BF16)
        return 0.25 * jnp.sum(low * low + high * high, axis=0, keepdims=True)

    wait_bytes(gath_a.at[pl.ds(0, na - 1)], gsem.at[3])
    sq_i = [unpack(gath_a, x_ref, k) for k in range(ki)]
    wait_bytes(gath_b.at[pl.ds(0, nb - 1)], gsem.at[1])
    sq_j = [unpack(gath_b, y_ref, k) for k in range(kj)]

    def upright(line):
        return jnp.broadcast_to(line, (LANES, LANES)).T

    def lanes(k):
        return slice(k * LANES, (k + 1) * LANES)

    def build(out, tall, sq_tall, wide, sq_wide):
        for k, line in enumerate(sq_tall):
            cross = lax.dot_general(
                tall[0:feats, lanes(k)], wide[0:feats, :], (((0,), (0,)), ((), ())), preferred_element_type=F32
            )
            up = upright(line)
            for s, other in enumerate(sq_wide):
                out[s, lanes(k), :] = LOG2E * (0.5 * cross[:, lanes(s)] - (up + other))

    STEP = 16

    def lse_pass(i, tile, vector):
        chunks, height = tile.shape[0], tile.shape[1]
        cols = None if vector is None else lines(vector)
        for k in range(height // LANES):
            tops, sums = [], []
            for h in range(k * LANES, (k + 1) * LANES, STEP):
                vs = [tile[s, h : h + STEP, :] for s in range(chunks)]
                if cols is not None:
                    vs = [v + c for v, c in zip(vs, cols)]
                top = tree(vs, jnp.maximum)
                tops.append(top)
                sums.append(tree([jnp.exp2(v - top) for v in vs], add))
            top = jnp.concatenate(tops, axis=0).T
            total = jnp.concatenate(sums, axis=0).T
            best = jnp.max(top, axis=0, keepdims=True)
            total = jnp.sum(total * jnp.exp2(top - best), axis=0, keepdims=True)
            mine[i, k : k + 1, :] = best + jnp.log2(total)

    def post(i, peers):
        for s, (dev, _) in enumerate(peers):
            send(mine.at[i], slots.at[i, s], ssem.at[i], rsem.at[i], dev)

    def arrive(i, peers):
        n = len(peers)
        wait_bytes(slots.at[i, pl.ds(0, n)], rsem.at[i])
        return [mine[i]] + [slots[i, s] for s in range(n)]

    def tree(parts, op):
        while len(parts) > 1:
            parts = [op(parts[t], parts[t + 1]) if t + 1 < len(parts) else parts[t] for t in range(0, len(parts), 2)]
        return parts[0]

    def add(u, v):
        return u + v

    def lse_end(i, peers):
        parts = arrive(i, peers)
        top = tree(parts, jnp.maximum)
        return -(top + jnp.log2(tree([jnp.exp2(p - top) for p in parts], add)))

    def lines(vector):
        return [vector[s : s + 1, :] for s in range(vector.shape[0])]

    build(c_ref, x_ref, sq_i, y_ref, sq_j)
    lse_pass(LR1, c_ref, None)
    post(LR1, peers_a)
    build(ct_ref, y_ref, sq_j, x_ref, sq_i)
    pot_row = lse_end(LR1, peers_a)
    lse_pass(LC1, ct_ref, pot_row)
    post(LC1, peers_b)
    pot_col = lse_end(LC1, peers_b)
    lse_pass(LR2, c_ref, pot_col)
    post(LR2, peers_a)
    pot_row = lse_end(LR2, peers_a)
    lse_pass(LC2, ct_ref, pot_row)
    post(LC2, peers_b)
    for k, line in enumerate(lines(pot_row)):
        fe_ref[lanes(k), :] = upright(line)
    pot_col = lse_end(LC2, peers_b)

    cols = lines(pot_col)
    for k in range(ki):
        totals = []
        for h in range(k * LANES, (k + 1) * LANES, STEP):
            up = fe_ref[h : h + STEP, :]
            parts = []
            for s in range(kj):
                e = jnp.exp2((up + cols[s]) + c_ref[s, h : h + STEP, :]).astype(BF16)
                p_ref[h : h + STEP, lanes(s)] = e
                parts.append(e.astype(F32))
            totals.append(tree(parts, add))
        mine[MASS, k : k + 1, :] = jnp.sum(jnp.concatenate(totals, axis=0).T, axis=0, keepdims=True)
    post(MASS, peers_a)

    def wide_dot(left):
        return jnp.dot(left, p_ref[...], preferred_element_type=F32)

    def tall_dot(left):
        return lax.dot_general(left, p_ref[...], (((1,), (1,)), ((), ())), preferred_element_type=F32)

    xp_ref[...] = wide_dot(x_ref[...])
    for s in range(kj):
        mine[CMASS, s : s + 1, :] = xp_ref[feats : feats + 1, lanes(s)]
    post(CMASS, peers_b)
    yp_ref[...] = tall_dot(y_ref[...])
    wait_bytes(gsl_a.at[pl.ds(0, na - 1)], gsem.at[7])
    wait_bytes(gsl_b.at[pl.ds(0, nb - 1)], gsem.at[5])
    for k in range(ki):
        row_ref[k : k + 1, :] = jnp.where(first1, gsl_a[2 * k], gsl_a[2 * k + 1])
    grad_f = row_ref[0:ki, :]
    for k in range(kj):
        row_ref[k : k + 1, :] = jnp.where(first1, gsl_b[2 * k], gsl_b[2 * k + 1])
    grad_g = row_ref[0:kj, :]

    def load_lhs(vector, width):
        high = vector.astype(BF16).astype(F32)
        rest = vector - high
        mid = rest.astype(BF16).astype(F32)
        low = rest - mid
        for s in range(width // LANES):
            lhs_ref[0:1, lanes(s)] = high[s : s + 1, :]
            lhs_ref[1:2, lanes(s)] = mid[s : s + 1, :]
            lhs_ref[2:3, lanes(s)] = low[s : s + 1, :]
        return lhs_ref[:, 0:width].astype(BF16)

    def keep(i, got):
        got = got[0:1] + got[1:2] + got[2:3]
        for s in range(got.shape[1] // LANES):
            mine[i, s : s + 1, :] = got[:, lanes(s)]

    def row_dot(i, vector):
        keep(i, tall_dot(load_lhs(vector, tj)))
        post(i, peers_a)

    def col_dot(i, vector):
        keep(i, wide_dot(load_lhs(vector, ti)))
        post(i, peers_b)

    row_mass = tree(arrive(MASS, peers_a), add)
    col_dot(PULL, grad_f / row_mass)
    col_mass = tree(arrive(CMASS, peers_b), add)
    residual = grad_g - tree(arrive(PULL, peers_b), add)

    def line_sum(v):
        return jnp.sum(v, axis=0, keepdims=True)

    def extra_post(i, peers):
        for s, (dev, _) in enumerate(peers):
            send(emine.at[i], eslots.at[i, s], essem.at[i], ersem.at[i], dev)

    def extra_arrive(i, peers):
        n = len(peers)
        wait_bytes(eslots.at[i, pl.ds(0, n)], ersem.at[i])
        got = tree([emine[i]] + [eslots[i, s] for s in range(n)], add)
        return jnp.sum(got, axis=1, keepdims=True)

    def spread(points, pulled, part, k):
        grad = 2.0 * (points.astype(F32) * pulled[feats : feats + 1, :] - pulled[0:feats, :])
        low, high = grad[0:half], grad[half:feats]
        part[2 * k] = jnp.where(first, low, pltpu.roll(high, pts, 1)).astype(BF16)
        part[2 * k + 1] = jnp.where(first, pltpu.roll(low, pts, 1), high).astype(BF16)

    def split(out, points, factors):
        rows = points.shape[0]
        for s, factor in enumerate(factors):
            v = points[:, lanes(s)].astype(F32) * factor
            high = v.astype(BF16)
            out[0:rows, lanes(s)] = high
            out[rows : 2 * rows, lanes(s)] = (v - high.astype(F32)).astype(BF16)

    rows = feats + 16

    def tgt_parts(g, us, ws, between):
        split(xu_ref, x_ref, us)
        got = wide_dot(xu_ref[...])
        between()
        for k in range(kj):
            pulled = got[0:rows, lanes(k)] + got[rows:, lanes(k)] + ws[k] * xp_ref[:, lanes(k)]
            spread(y_ref[0:feats, lanes(k)], pulled, part_b.at[g], k)
        for s, (dev, peer) in enumerate(peers_b):
            send(part_b.at[g, peer], rs_b.at[g, s], sgb.at[g], rgb.at[g], dev)

    def src_parts(g, us, pulled_of):
        for k in range(ki):
            spread(x_ref[0:feats, lanes(k)], pulled_of(k) + us[k] * yp_ref[:, lanes(k)], part_a.at[g], k)
        for s, (dev, peer) in enumerate(peers_a):
            send(part_a.at[g, peer], rs_a.at[g, s], sga.at[g], rga.at[g], dev)

    def early_gradients(on_row, on_col, residual, direction):
        us, ws = lines(on_row), lines(on_col)
        for t, vector in enumerate((on_col, residual, direction)):
            split(yw_ref.at[pl.ds(2 * rows * t, 2 * rows)], y_ref, lines(vector))
        got = tall_dot(yw_ref[...])
        for t in range(1, 3):
            at = 2 * rows * t
            yk_ref[t - 1] = got[at : at + rows] + got[at + rows : at + 2 * rows]

        def between():
            src_parts(0, us, lambda k: got[0:rows, lanes(k)] + got[rows : 2 * rows, lanes(k)])

        tgt_parts(0, us, ws, between)

    def late_gradients(on_row, on_col, beta):
        us, ws = lines(on_row), lines(on_col)

        def between():
            src_parts(1, us, lambda k: yk_ref[0, :, lanes(k)] + beta * yk_ref[1, :, lanes(k)])

        tgt_parts(1, us, ws, between)

    dual = pulled_dual = direction = applied = norm = d_c_d = None
    for it in range(CG):
        i_a, i_b = A1 + 2 * it, A1 + 2 * it + 1
        e_a, e_b = 2 * it, 2 * it + 1
        weighted = col_mass * residual
        emine[e_a, 0:1, :] = line_sum(residual * residual)
        emine[e_a, 1:2, :] = line_sum(weighted * residual)
        if it:
            emine[e_a, 2:3, :] = line_sum(weighted * direction)
        extra_post(e_a, peers_a)
        row_dot(i_a, residual)
        if it == CG - 1:
            early_gradients((grad_f - pulled_dual) / row_mass, dual, residual, direction)
        scal = extra_arrive(e_a, peers_a)
        fresh = tree(arrive(i_a, peers_a), add)
        if it:
            beta = scal[0:1] / norm
            direction = residual + beta * direction
            applied = fresh + beta * applied
            d_c_d = scal[1:2] + 2.0 * beta * scal[2:3] + beta * beta * d_c_d
        else:
            direction, applied, d_c_d = residual, fresh, scal[1:2]
        norm = scal[0:1]
        back = applied / row_mass
        emine[e_b, 0:1, :] = line_sum(applied * back)
        extra_post(e_b, peers_b)
        if it == CG - 1:
            late_gradients(-back, direction, beta)
            q_q = extra_arrive(e_b, peers_b)[0:1]
            alpha = norm / ((1.0 + TAU) * d_c_d - q_q)
            continue
        col_dot(i_b, back)
        q_q = extra_arrive(e_b, peers_b)[0:1]
        alpha = norm / ((1.0 + TAU) * d_c_d - q_q)
        dual = alpha * direction if it == 0 else dual + alpha * direction
        pulled_dual = alpha * applied if it == 0 else pulled_dual + alpha * applied
        image = (1.0 + TAU) * col_mass * direction - tree(arrive(i_b, peers_b), add)
        residual = residual - alpha * image

    def collect(g, part, me, slot, n, sem):
        wait_bytes(slot.at[g], sem.at[g])
        return tree([part[g, me].astype(F32)] + [slot[g, s].astype(F32) for s in range(n)], add)

    def store(out, got):
        out[0:half, :] = got[:, 0:pts]
        out[half:feats, :] = got[:, pts:]

    base_a = collect(0, part_a, me_a, rs_a, na - 1, rga)
    base_b = collect(0, part_b, me_b, rs_b, nb - 1, rgb)
    store(osrc_ref, base_a + alpha * collect(1, part_a, me_a, rs_a, na - 1, rga))
    store(otgt_ref, base_b + alpha * collect(1, part_b, me_b, rs_b, nb - 1, rgb))

    wait_bytes(gath_b.at[pl.ds(0, nb - 1)], gsem.at[0])
    wait_bytes(gath_a.at[pl.ds(0, na - 1)], gsem.at[2])
    wait_bytes(gsl_b.at[pl.ds(0, nb - 1)], gsem.at[4])
    wait_bytes(gsl_a.at[pl.ds(0, na - 1)], gsem.at[6])
    for g in range(2):
        wait_bytes(rs_a.at[g], sga.at[g])
        wait_bytes(rs_b.at[g], sgb.at[g])
    over_a = (LR1, LR2, MASS, A1, A1 + 2, A1 + 4)
    for i in range(ROUNDS):
        wait_bytes(slots.at[i, pl.ds(0, len(peers_a if i in over_a else peers_b))], ssem.at[i])
    for e in range(2 * CG):
        wait_bytes(eslots.at[e, pl.ds(0, len(peers_a if e % 2 == 0 else peers_b))], essem.at[e])


def body(sizes, src_points, tgt_points, grad_f, grad_g):
    nx, ny, nz, nc = sizes
    feats, pts = src_points.shape
    na, nb = nx * ny, nz * nc
    ti, tj = na * pts, nb * pts
    ki, kj = ti // LANES, tj // LANES
    n = max(na, nb) - 1
    k = max(ki, kj)
    half = feats // 2
    rows = feats + 16
    vmem = pl.BlockSpec(memory_space=pltpu.VMEM)
    out = jax.ShapeDtypeStruct((feats, pts), F32)
    return pl.pallas_call(
        functools.partial(kernel, sizes),
        out_shape=(out, out),
        in_specs=[pl.BlockSpec(memory_space=pl.ANY)] * 4,
        out_specs=(vmem, vmem),
        scratch_shapes=[
            pltpu.VMEM((feats, pts), BF16),
            pltpu.VMEM((feats, pts), BF16),
            pltpu.VMEM((grad_f.shape[0] // LANES, LANES), F32),
            pltpu.VMEM((grad_g.shape[0] // LANES, LANES), F32),
            pltpu.VMEM((half, LANES), BF16),
            pltpu.VMEM((half, LANES), BF16),
            pltpu.VMEM((na, half, LANES), BF16),
            pltpu.VMEM((nb, half, LANES), BF16),
            pltpu.VMEM((1, LANES), F32),
            pltpu.VMEM((1, LANES), F32),
            pltpu.VMEM((na, 1, LANES), F32),
            pltpu.VMEM((nb, 1, LANES), F32),
            pltpu.VMEM((rows, ti), BF16),
            pltpu.VMEM((rows, tj), BF16),
            pltpu.VMEM((kj, ti, LANES), F32),
            pltpu.VMEM((ki, tj, LANES), F32),
            pltpu.VMEM((ti, tj), BF16),
            pltpu.VMEM((ti, LANES), F32),
            pltpu.VMEM((8, max(ti, tj)), F32),
            pltpu.VMEM((k, LANES), F32),
            pltpu.VMEM((2 * rows, ti), BF16),
            pltpu.VMEM((6 * rows, tj), BF16),
            pltpu.VMEM((rows, tj), F32),
            pltpu.VMEM((rows, ti), F32),
            pltpu.VMEM((2, rows, ti), F32),
            pltpu.VMEM((ROUNDS, k, LANES), F32),
            pltpu.VMEM((ROUNDS, n, k, LANES), F32),
            pltpu.VMEM((2 * CG, 4, LANES), F32),
            pltpu.VMEM((2 * CG, n, 4, LANES), F32),
            pltpu.VMEM((2, na, half, LANES), BF16),
            pltpu.VMEM((2, nb, half, LANES), BF16),
            pltpu.VMEM((2, na - 1, half, LANES), BF16),
            pltpu.VMEM((2, nb - 1, half, LANES), BF16),
            pltpu.SemaphoreType.DMA((4,)),
            pltpu.SemaphoreType.DMA((8,)),
            pltpu.SemaphoreType.DMA((ROUNDS,)),
            pltpu.SemaphoreType.DMA((ROUNDS,)),
            pltpu.SemaphoreType.DMA((2 * CG,)),
            pltpu.SemaphoreType.DMA((2 * CG,)),
            pltpu.SemaphoreType.DMA((2,)),
            pltpu.SemaphoreType.DMA((2,)),
            pltpu.SemaphoreType.DMA((2,)),
            pltpu.SemaphoreType.DMA((2,)),
        ],
        compiler_params=pltpu.CompilerParams(
            collective_id=0, has_side_effects=True, vmem_limit_bytes=40 * 1024 * 1024
        ),
        name="transport",
    )(src_points, tgt_points, grad_f.reshape(-1, LANES), grad_g.reshape(-1, LANES))

def solution(mesh):
    rows, cols = mesh.shape["row"], mesh.shape["col"]
    sizes = (4, cols // 4, rows // 2, 2)
    in_specs = (P(None, ("row", "col")), P(None, ("col", "row")), P("row"), P("col"))
    out_specs = (P(None, ("row", "col")), P(None, ("col", "row")))
    return jax.shard_map(
        functools.partial(body, sizes), mesh=mesh, in_specs=in_specs, out_specs=out_specs, check_vma=False
    )
```

```python
import functools
import math

import jax
import jax.numpy as jnp
from jax import lax
from jax.experimental import pallas as pl
from jax.experimental.pallas import tpu as pltpu
from jax.sharding import PartitionSpec as P

CG = 3
TAU = 0.1
LOG2E = math.log2(math.e)
LANES = 128
MESH = pl.DeviceIdType.MESH
F32 = jnp.float32
BF16 = jnp.bfloat16

LR1, LC1, LR2, LC2, MASS, PULL, CMASS, A1 = range(8)
ROUNDS = 12


def ring(d, n):
    return min(d % n, n - d % n)


def kernel(
    sizes, src_hbm, tgt_hbm, gf_hbm, gg_hbm, osrc_ref, otgt_ref,
    src_ref, tgt_ref, gf_ref, gg_ref,
    pack_a, pack_b, gath_a, gath_b, gown_a, gown_b, gsl_a, gsl_b,
    x_ref, y_ref, c_ref, ct_ref, p_ref, fe_ref, lhs_ref, row_ref, xu_ref, yw_ref, xp_ref, yp_ref, yk_ref,
    mine, slots, emine, eslots, part_a, part_b, rs_a, rs_b,
    isem, gsem, ssem, rsem, essem, ersem, sga, rga, sgb, rgb,
):
    nx, ny, nz, nc = sizes
    na, nb = nx * ny, nz * nc
    row, col = lax.axis_index("row"), lax.axis_index("col")
    z, x_lo = row // 2, row % 2
    x_hi, y, core = col // (2 * ny), (col // 2) % ny, col % 2
    x = x_hi * 2 + x_lo
    me_a, me_b = x * ny + y, z * nc + core
    feats, pts = src_ref.shape
    half = feats // 2
    ti, tj = na * pts, nb * pts
    ki, kj = ti // LANES, tj // LANES

    offs_a = [(i, j) for i in range(nx) for j in range(ny) if i or j]
    offs_a.sort(key=lambda o: -(ring(o[0], nx) + ring(o[1], ny)))
    offs_b = [(i, j) for i in range(nz) for j in range(nc) if i or j]
    offs_b.sort(key=lambda o: -(ring(o[0], nz) + 0.1 * o[1]))
    peers_a, peers_b = [], []
    for dx, dy in offs_a:
        px, py = (x + dx) % nx, (y + dy) % ny
        peers_a.append(((z * 2 + px % 2, (px // 2) * (2 * ny) + py * 2 + core), px * ny + py))
    for dz, dc in offs_b:
        pz, pc = (z + dz) % nz, (core + dc) % nc
        peers_b.append(((pz * 2 + x_lo, x_hi * (2 * ny) + y * 2 + pc), pz * nc + pc))

    def send(src, dst, s_sem, r_sem, dev):
        pltpu.make_async_remote_copy(
            src_ref=src, dst_ref=dst, send_sem=s_sem, recv_sem=r_sem, device_id=dev, device_id_type=MESH
        ).start()

    def wait_bytes(ref, sem):
        pltpu.make_async_copy(ref, ref, sem).wait()

    barrier = pltpu.get_barrier_semaphore()
    for dev, _ in peers_a + peers_b:
        pl.semaphore_signal(barrier, inc=1, device_id=dev, device_id_type=MESH)
    loads = [
        pltpu.make_async_copy(here, there, isem.at[n])
        for n, (here, there) in enumerate(
            ((src_hbm, src_ref), (tgt_hbm, tgt_ref), (gf_hbm, gf_ref), (gg_hbm, gg_ref))
        )
    ]
    for load in loads:
        load.start()

    first = lax.broadcasted_iota(jnp.int32, (half, LANES), 1) < pts
    first1 = lax.broadcasted_iota(jnp.int32, (1, LANES), 1) < pts
    lhs_ref[...] = jnp.zeros_like(lhs_ref)
    emine[...] = jnp.zeros_like(emine)
    for ref in (x_ref, y_ref):
        pad = (ref.shape[0] - feats, ref.shape[1])
        ref[feats:, :] = (lax.broadcasted_iota(jnp.int32, pad, 0) == 0).astype(F32).astype(BF16)

    def pack(block):
        return jnp.concatenate([block[:half], block[half:]], axis=1).astype(BF16)

    def own(ref, at):
        line = ref[pl.ds(at // 2, 1), :]
        other = pltpu.roll(line, pts, 1)
        here = at % 2
        low = jnp.where(here == 0, line, other)
        high = jnp.where(here == 0, other, line)
        return jnp.where(first1, low, high)

    for load in loads:
        load.wait()
    pack_a[...] = pack(src_ref[...].astype(F32))
    pack_b[...] = pack(tgt_ref[...].astype(F32))
    gown_a[...] = own(gf_ref, col)
    gown_b[...] = own(gg_ref, row)
    gath_a[me_a] = pack_a[...]
    gath_b[me_b] = pack_b[...]
    gsl_a[me_a] = gown_a[...]
    gsl_b[me_b] = gown_b[...]
    pl.semaphore_wait(barrier, na + nb - 2)

    for dev, _ in peers_b:
        send(pack_b, gath_b.at[me_b], gsem.at[0], gsem.at[1], dev)
    for dev, _ in peers_a:
        send(pack_a, gath_a.at[me_a], gsem.at[2], gsem.at[3], dev)
    for dev, _ in peers_b:
        send(gown_b, gsl_b.at[me_b], gsem.at[4], gsem.at[5], dev)
    for dev, _ in peers_a:
        send(gown_a, gsl_a.at[me_a], gsem.at[6], gsem.at[7], dev)

    def unpack(gath, out, k):
        one, two = gath[2 * k].astype(F32), gath[2 * k + 1].astype(F32)
        at = slice(k * LANES, (k + 1) * LANES)
        low = jnp.where(first, one, pltpu.roll(two, pts, 1))
        high = jnp.where(first, pltpu.roll(one, pts, 1), two)
        out[0:half, at] = low.astype(BF16)
        out[half:feats, at] = high.astype(BF16)
        return 0.25 * jnp.sum(low * low + high * high, axis=0, keepdims=True)

    wait_bytes(gath_a.at[pl.ds(0, na - 1)], gsem.at[3])
    sq_i = [unpack(gath_a, x_ref, k) for k in range(ki)]
    wait_bytes(gath_b.at[pl.ds(0, nb - 1)], gsem.at[1])
    sq_j = [unpack(gath_b, y_ref, k) for k in range(kj)]

    def upright(line):
        return jnp.broadcast_to(line, (LANES, LANES)).T

    def lanes(k):
        return slice(k * LANES, (k + 1) * LANES)

    def build(out, tall, sq_tall, wide, sq_wide):
        for k, line in enumerate(sq_tall):
            cross = lax.dot_general(
                tall[0:feats, lanes(k)], wide[0:feats, :], (((0,), (0,)), ((), ())), preferred_element_type=F32
            )
            up = upright(line)
            for s, other in enumerate(sq_wide):
                out[s, lanes(k), :] = LOG2E * (0.5 * cross[:, lanes(s)] - (up + other))

    STEP = 16

    def lse_pass(i, tile, vector):
        chunks, height = tile.shape[0], tile.shape[1]
        cols = None if vector is None else lines(vector)
        for k in range(height // LANES):
            tops, sums = [], []
            for h in range(k * LANES, (k + 1) * LANES, STEP):
                vs = [tile[s, h : h + STEP, :] for s in range(chunks)]
                if cols is not None:
                    vs = [v + c for v, c in zip(vs, cols)]
                top = tree(vs, jnp.maximum)
                tops.append(top)
                sums.append(tree([jnp.exp2(v - top) for v in vs], add))
            top = jnp.concatenate(tops, axis=0).T
            total = jnp.concatenate(sums, axis=0).T
            best = jnp.max(top, axis=0, keepdims=True)
            total = jnp.sum(total * jnp.exp2(top - best), axis=0, keepdims=True)
            mine[i, k : k + 1, :] = best + jnp.log2(total)

    def post(i, peers):
        for s, (dev, _) in enumerate(peers):
            send(mine.at[i], slots.at[i, s], ssem.at[i], rsem.at[i], dev)

    def arrive(i, peers):
        n = len(peers)
        wait_bytes(slots.at[i, pl.ds(0, n)], rsem.at[i])
        return [mine[i]] + [slots[i, s] for s in range(n)]

    def tree(parts, op):
        while len(parts) > 1:
            parts = [op(parts[t], parts[t + 1]) if t + 1 < len(parts) else parts[t] for t in range(0, len(parts), 2)]
        return parts[0]

    def add(u, v):
        return u + v

    def lse_end(i, peers):
        parts = arrive(i, peers)
        top = tree(parts, jnp.maximum)
        return -(top + jnp.log2(tree([jnp.exp2(p - top) for p in parts], add)))

    def lines(vector):
        return [vector[s : s + 1, :] for s in range(vector.shape[0])]

    build(c_ref, x_ref, sq_i, y_ref, sq_j)
    lse_pass(LR1, c_ref, None)
    post(LR1, peers_a)
    build(ct_ref, y_ref, sq_j, x_ref, sq_i)
    pot_row = lse_end(LR1, peers_a)
    lse_pass(LC1, ct_ref, pot_row)
    post(LC1, peers_b)
    pot_col = lse_end(LC1, peers_b)
    lse_pass(LR2, c_ref, pot_col)
    post(LR2, peers_a)
    pot_row = lse_end(LR2, peers_a)
    lse_pass(LC2, ct_ref, pot_row)
    post(LC2, peers_b)
    for k, line in enumerate(lines(pot_row)):
        fe_ref[lanes(k), :] = upright(line)
    pot_col = lse_end(LC2, peers_b)

    cols = lines(pot_col)
    for k in range(ki):
        totals = []
        for h in range(k * LANES, (k + 1) * LANES, STEP):
            up = fe_ref[h : h + STEP, :]
            parts = []
            for s in range(kj):
                e = jnp.exp2((up + cols[s]) + c_ref[s, h : h + STEP, :]).astype(BF16)
                p_ref[h : h + STEP, lanes(s)] = e
                parts.append(e.astype(F32))
            totals.append(tree(parts, add))
        mine[MASS, k : k + 1, :] = jnp.sum(jnp.concatenate(totals, axis=0).T, axis=0, keepdims=True)
    post(MASS, peers_a)

    def wide_dot(left):
        return jnp.dot(left, p_ref[...], preferred_element_type=F32)

    def tall_dot(left):
        return lax.dot_general(left, p_ref[...], (((1,), (1,)), ((), ())), preferred_element_type=F32)

    xp_ref[...] = wide_dot(x_ref[...])
    for s in range(kj):
        mine[CMASS, s : s + 1, :] = xp_ref[feats : feats + 1, lanes(s)]
    post(CMASS, peers_b)
    yp_ref[...] = tall_dot(y_ref[...])
    wait_bytes(gsl_a.at[pl.ds(0, na - 1)], gsem.at[7])
    wait_bytes(gsl_b.at[pl.ds(0, nb - 1)], gsem.at[5])
    for k in range(ki):
        row_ref[k : k + 1, :] = jnp.where(first1, gsl_a[2 * k], gsl_a[2 * k + 1])
    grad_f = row_ref[0:ki, :]
    for k in range(kj):
        row_ref[k : k + 1, :] = jnp.where(first1, gsl_b[2 * k], gsl_b[2 * k + 1])
    grad_g = row_ref[0:kj, :]

    def load_lhs(vector, width):
        high = vector.astype(BF16).astype(F32)
        rest = vector - high
        mid = rest.astype(BF16).astype(F32)
        low = rest - mid
        for s in range(width // LANES):
            lhs_ref[0:1, lanes(s)] = high[s : s + 1, :]
            lhs_ref[1:2, lanes(s)] = mid[s : s + 1, :]
            lhs_ref[2:3, lanes(s)] = low[s : s + 1, :]
        return lhs_ref[:, 0:width].astype(BF16)

    def keep(i, got):
        got = got[0:1] + got[1:2] + got[2:3]
        for s in range(got.shape[1] // LANES):
            mine[i, s : s + 1, :] = got[:, lanes(s)]

    def row_dot(i, vector):
        keep(i, tall_dot(load_lhs(vector, tj)))
        post(i, peers_a)

    def col_dot(i, vector):
        keep(i, wide_dot(load_lhs(vector, ti)))
        post(i, peers_b)

    row_mass = tree(arrive(MASS, peers_a), add)
    col_dot(PULL, grad_f / row_mass)
    col_mass = tree(arrive(CMASS, peers_b), add)
    residual = grad_g - tree(arrive(PULL, peers_b), add)

    def line_sum(v):
        return jnp.sum(v, axis=0, keepdims=True)

    def extra_post(i, peers):
        for s, (dev, _) in enumerate(peers):
            send(emine.at[i], eslots.at[i, s], essem.at[i], ersem.at[i], dev)

    def extra_arrive(i, peers):
        n = len(peers)
        wait_bytes(eslots.at[i, pl.ds(0, n)], ersem.at[i])
        got = tree([emine[i]] + [eslots[i, s] for s in range(n)], add)
        return jnp.sum(got, axis=1, keepdims=True)

    def spread(points, pulled, part, k):
        grad = 2.0 * (points.astype(F32) * pulled[feats : feats + 1, :] - pulled[0:feats, :])
        low, high = grad[0:half], grad[half:feats]
        part[2 * k] = jnp.where(first, low, pltpu.roll(high, pts, 1)).astype(BF16)
        part[2 * k + 1] = jnp.where(first, pltpu.roll(low, pts, 1), high).astype(BF16)

    def split(out, points, factors):
        rows = points.shape[0]
        for s, factor in enumerate(factors):
            v = points[:, lanes(s)].astype(F32) * factor
            high = v.astype(BF16)
            out[0:rows, lanes(s)] = high
            out[rows : 2 * rows, lanes(s)] = (v - high.astype(F32)).astype(BF16)

    rows = feats + 16

    def tgt_parts(g, us, ws, between):
        split(xu_ref, x_ref, us)
        got = wide_dot(xu_ref[...])
        between()
        for k in range(kj):
            pulled = got[0:rows, lanes(k)] + got[rows:, lanes(k)] + ws[k] * xp_ref[:, lanes(k)]
            spread(y_ref[0:feats, lanes(k)], pulled, part_b.at[g], k)
        for s, (dev, peer) in enumerate(peers_b):
            send(part_b.at[g, peer], rs_b.at[g, s], sgb.at[g], rgb.at[g], dev)

    def src_parts(g, us, pulled_of):
        for k in range(ki):
            spread(x_ref[0:feats, lanes(k)], pulled_of(k) + us[k] * yp_ref[:, lanes(k)], part_a.at[g], k)
        for s, (dev, peer) in enumerate(peers_a):
            send(part_a.at[g, peer], rs_a.at[g, s], sga.at[g], rga.at[g], dev)

    def early_gradients(on_row, on_col, residual, direction):
        us, ws = lines(on_row), lines(on_col)
        for t, vector in enumerate((on_col, residual, direction)):
            split(yw_ref.at[pl.ds(2 * rows * t, 2 * rows)], y_ref, lines(vector))
        got = tall_dot(yw_ref[...])
        for t in range(1, 3):
            at = 2 * rows * t
            yk_ref[t - 1] = got[at : at + rows] + got[at + rows : at + 2 * rows]

        def between():
            src_parts(0, us, lambda k: got[0:rows, lanes(k)] + got[rows : 2 * rows, lanes(k)])

        tgt_parts(0, us, ws, between)

    def late_gradients(on_row, on_col, beta):
        us, ws = lines(on_row), lines(on_col)

        def between():
            src_parts(1, us, lambda k: yk_ref[0, :, lanes(k)] + beta * yk_ref[1, :, lanes(k)])

        tgt_parts(1, us, ws, between)

    dual = pulled_dual = direction = applied = norm = d_c_d = None
    for it in range(CG):
        i_a, i_b = A1 + 2 * it, A1 + 2 * it + 1
        e_a, e_b = 2 * it, 2 * it + 1
        weighted = col_mass * residual
        emine[e_a, 0:1, :] = line_sum(residual * residual)
        emine[e_a, 1:2, :] = line_sum(weighted * residual)
        if it:
            emine[e_a, 2:3, :] = line_sum(weighted * direction)
        extra_post(e_a, peers_a)
        row_dot(i_a, residual)
        if it == CG - 1:
            early_gradients((grad_f - pulled_dual) / row_mass, dual, residual, direction)
        scal = extra_arrive(e_a, peers_a)
        fresh = tree(arrive(i_a, peers_a), add)
        if it:
            beta = scal[0:1] / norm
            direction = residual + beta * direction
            applied = fresh + beta * applied
            d_c_d = scal[1:2] + 2.0 * beta * scal[2:3] + beta * beta * d_c_d
        else:
            direction, applied, d_c_d = residual, fresh, scal[1:2]
        norm = scal[0:1]
        back = applied / row_mass
        emine[e_b, 0:1, :] = line_sum(applied * back)
        extra_post(e_b, peers_b)
        if it == CG - 1:
            late_gradients(-back, direction, beta)
            q_q = extra_arrive(e_b, peers_b)[0:1]
            alpha = norm / ((1.0 + TAU) * d_c_d - q_q)
            continue
        col_dot(i_b, back)
        q_q = extra_arrive(e_b, peers_b)[0:1]
        alpha = norm / ((1.0 + TAU) * d_c_d - q_q)
        dual = alpha * direction if it == 0 else dual + alpha * direction
        pulled_dual = alpha * applied if it == 0 else pulled_dual + alpha * applied
        image = (1.0 + TAU) * col_mass * direction - tree(arrive(i_b, peers_b), add)
        residual = residual - alpha * image

    def collect(g, part, me, slot, n, sem):
        wait_bytes(slot.at[g], sem.at[g])
        return tree([part[g, me].astype(F32)] + [slot[g, s].astype(F32) for s in range(n)], add)

    def store(out, got):
        out[0:half, :] = got[:, 0:pts]
        out[half:feats, :] = got[:, pts:]

    base_a = collect(0, part_a, me_a, rs_a, na - 1, rga)
    base_b = collect(0, part_b, me_b, rs_b, nb - 1, rgb)
    store(osrc_ref, base_a + alpha * collect(1, part_a, me_a, rs_a, na - 1, rga))
    store(otgt_ref, base_b + alpha * collect(1, part_b, me_b, rs_b, nb - 1, rgb))

    wait_bytes(gath_b.at[pl.ds(0, nb - 1)], gsem.at[0])
    wait_bytes(gath_a.at[pl.ds(0, na - 1)], gsem.at[2])
    wait_bytes(gsl_b.at[pl.ds(0, nb - 1)], gsem.at[4])
    wait_bytes(gsl_a.at[pl.ds(0, na - 1)], gsem.at[6])
    for g in range(2):
        wait_bytes(rs_a.at[g], sga.at[g])
        wait_bytes(rs_b.at[g], sgb.at[g])
    over_a = (LR1, LR2, MASS, A1, A1 + 2, A1 + 4)
    for i in range(ROUNDS):
        wait_bytes(slots.at[i, pl.ds(0, len(peers_a if i in over_a else peers_b))], ssem.at[i])
    for e in range(2 * CG):
        wait_bytes(eslots.at[e, pl.ds(0, len(peers_a if e % 2 == 0 else peers_b))], essem.at[e])


def hand_over(one_ref, two_ref, first_ref, second_ref):
    first_ref[...] = one_ref[...]
    second_ref[...] = two_ref[...]


def body(sizes, src_points, tgt_points, grad_f, grad_g):
    nx, ny, nz, nc = sizes
    feats, pts = src_points.shape
    na, nb = nx * ny, nz * nc
    ti, tj = na * pts, nb * pts
    ki, kj = ti // LANES, tj // LANES
    n = max(na, nb) - 1
    k = max(ki, kj)
    half = feats // 2
    rows = feats + 16
    vmem = pl.BlockSpec(memory_space=pltpu.VMEM)
    out = jax.ShapeDtypeStruct((feats, pts), F32)
    both = pl.pallas_call(
        functools.partial(kernel, sizes),
        out_shape=(out, out),
        in_specs=[pl.BlockSpec(memory_space=pl.ANY)] * 4,
        out_specs=(vmem, vmem),
        scratch_shapes=[
            pltpu.VMEM((feats, pts), BF16),
            pltpu.VMEM((feats, pts), BF16),
            pltpu.VMEM((grad_f.shape[0] // LANES, LANES), F32),
            pltpu.VMEM((grad_g.shape[0] // LANES, LANES), F32),
            pltpu.VMEM((half, LANES), BF16),
            pltpu.VMEM((half, LANES), BF16),
            pltpu.VMEM((na, half, LANES), BF16),
            pltpu.VMEM((nb, half, LANES), BF16),
            pltpu.VMEM((1, LANES), F32),
            pltpu.VMEM((1, LANES), F32),
            pltpu.VMEM((na, 1, LANES), F32),
            pltpu.VMEM((nb, 1, LANES), F32),
            pltpu.VMEM((rows, ti), BF16),
            pltpu.VMEM((rows, tj), BF16),
            pltpu.VMEM((kj, ti, LANES), F32),
            pltpu.VMEM((ki, tj, LANES), F32),
            pltpu.VMEM((ti, tj), BF16),
            pltpu.VMEM((ti, LANES), F32),
            pltpu.VMEM((8, max(ti, tj)), F32),
            pltpu.VMEM((k, LANES), F32),
            pltpu.VMEM((2 * rows, ti), BF16),
            pltpu.VMEM((6 * rows, tj), BF16),
            pltpu.VMEM((rows, tj), F32),
            pltpu.VMEM((rows, ti), F32),
            pltpu.VMEM((2, rows, ti), F32),
            pltpu.VMEM((ROUNDS, k, LANES), F32),
            pltpu.VMEM((ROUNDS, n, k, LANES), F32),
            pltpu.VMEM((2 * CG, 4, LANES), F32),
            pltpu.VMEM((2 * CG, n, 4, LANES), F32),
            pltpu.VMEM((2, na, half, LANES), BF16),
            pltpu.VMEM((2, nb, half, LANES), BF16),
            pltpu.VMEM((2, na - 1, half, LANES), BF16),
            pltpu.VMEM((2, nb - 1, half, LANES), BF16),
            pltpu.SemaphoreType.DMA((4,)),
            pltpu.SemaphoreType.DMA((8,)),
            pltpu.SemaphoreType.DMA((ROUNDS,)),
            pltpu.SemaphoreType.DMA((ROUNDS,)),
            pltpu.SemaphoreType.DMA((2 * CG,)),
            pltpu.SemaphoreType.DMA((2 * CG,)),
            pltpu.SemaphoreType.DMA((2,)),
            pltpu.SemaphoreType.DMA((2,)),
            pltpu.SemaphoreType.DMA((2,)),
            pltpu.SemaphoreType.DMA((2,)),
        ],
        compiler_params=pltpu.CompilerParams(
            collective_id=0, has_side_effects=True, vmem_limit_bytes=56 * 1024 * 1024
        ),
        name="transport",
    )(src_points, tgt_points, grad_f.reshape(-1, LANES), grad_g.reshape(-1, LANES))
    return pl.pallas_call(
        hand_over, out_shape=(out, out), in_specs=[vmem] * 2, out_specs=(vmem, vmem), name="hand_over"
    )(*both)


def solution(mesh):
    rows, cols = mesh.shape["row"], mesh.shape["col"]
    sizes = (4, cols // 4, rows // 2, 2)
    in_specs = (P(None, ("row", "col")), P(None, ("col", "row")), P("row"), P("col"))
    out_specs = (P(None, ("row", "col")), P(None, ("col", "row")))
    return jax.shard_map(
        functools.partial(body, sizes), mesh=mesh, in_specs=in_specs, out_specs=out_specs, check_vma=False
    )
```

```python
import functools
import math

import jax
import jax.numpy as jnp
from jax import lax
from jax.experimental import pallas as pl
from jax.experimental.pallas import tpu as pltpu
from jax.sharding import PartitionSpec as P

CG = 3
TAU = 0.1
LOG2E = math.log2(math.e)
LANES = 128
MESH = pl.DeviceIdType.MESH
F32 = jnp.float32
BF16 = jnp.bfloat16

LR1, LC1, LR2, LC2, MASS, PULL, CMASS, A1 = range(8)
ROUNDS = 12


def ring(d, n):
    return min(d % n, n - d % n)


def kernel(
    sizes, src_hbm, tgt_hbm, gf_hbm, gg_hbm, osrc_ref, otgt_ref,
    src_ref, tgt_ref, gf_ref, gg_ref,
    pack_a, pack_b, gath_a, gath_b, gown_a, gown_b, gsl_a, gsl_b,
    x_ref, y_ref, c_ref, ct_ref, p_ref, fe_ref, lhs_ref, row_ref, xu_ref, yw_ref, xp_ref, yp_ref, yk_ref,
    mine, slots, hmine, hslots, top_ref, sum_ref, emine, eslots, part_a, part_b, rs_a, rs_b,
    isem, gsem, hsem, hrsem, ssem, rsem, essem, ersem, sga, rga, sgb, rgb,
):
    nx, ny, nz, nc = sizes
    na, nb = nx * ny, nz * nc
    row, col = lax.axis_index("row"), lax.axis_index("col")
    z, x_lo = lax.div(row, 2), lax.rem(row, 2)
    x_hi, y, core = lax.div(col, 2 * ny), lax.rem(lax.div(col, 2), ny), lax.rem(col, 2)
    x = x_hi * 2 + x_lo
    me_a, me_b = x * ny + y, z * nc + core
    feats, pts = src_ref.shape
    half = feats // 2
    ti, tj = na * pts, nb * pts
    ki, kj = ti // LANES, tj // LANES

    offs_a = [(i, j) for i in range(nx) for j in range(ny) if i or j]
    offs_a.sort(key=lambda o: -(ring(o[0], nx) + ring(o[1], ny)))
    offs_b = [(i, j) for i in range(nz) for j in range(nc) if i or j]
    offs_b.sort(key=lambda o: -(ring(o[0], nz) + 0.1 * o[1]))
    peers_a, peers_b = [], []
    xs = [lax.rem(x + d, nx) for d in range(nx)]
    xs = [(z * 2 + lax.rem(p, 2), lax.div(p, 2) * (2 * ny) + core, p * ny) for p in xs]
    ys = [lax.rem(y + d, ny) for d in range(ny)]
    zs = [lax.rem(z + d, nz) for d in range(nz)]
    zs = [(p * 2 + x_lo, p * nc) for p in zs]
    cs = [(col - core + p, p) for p in (core, 1 - core)]
    for dx, dy in offs_a:
        peers_a.append(((xs[dx][0], xs[dx][1] + ys[dy] * 2), xs[dx][2] + ys[dy]))
    for dz, dc in offs_b:
        peers_b.append(((zs[dz][0], cs[dc][0]), zs[dz][1] + cs[dc][1]))

    def send(src, dst, s_sem, r_sem, dev):
        pltpu.make_async_remote_copy(
            src_ref=src, dst_ref=dst, send_sem=s_sem, recv_sem=r_sem, device_id=dev, device_id_type=MESH
        ).start()

    def wait_bytes(ref, sem):
        pltpu.make_async_copy(ref, ref, sem).wait()

    barrier = pltpu.get_barrier_semaphore()
    for dev, _ in peers_b + peers_a:
        pl.semaphore_signal(barrier, inc=1, device_id=dev, device_id_type=MESH)
    loads = [
        pltpu.make_async_copy(here, there, isem.at[n])
        for n, (here, there) in enumerate(
            ((src_hbm, src_ref), (tgt_hbm, tgt_ref), (gf_hbm, gf_ref), (gg_hbm, gg_ref))
        )
    ]
    for load in loads:
        load.start()

    first = lax.broadcasted_iota(jnp.int32, (half, LANES), 1) < pts
    first1 = lax.broadcasted_iota(jnp.int32, (1, LANES), 1) < pts
    lhs_ref[...] = jnp.zeros_like(lhs_ref)
    emine[...] = jnp.zeros_like(emine)
    for ref in (x_ref, y_ref):
        pad = (ref.shape[0] - feats, ref.shape[1])
        ref[feats:, :] = (lax.broadcasted_iota(jnp.int32, pad, 0) == 0).astype(F32).astype(BF16)

    def pack(block):
        return jnp.concatenate([block[:half], block[half:]], axis=1).astype(BF16)

    def own(ref, at):
        line = ref[pl.ds(lax.div(at, 2), 1), :]
        other = pltpu.roll(line, pts, 1)
        here = lax.rem(at, 2)
        low = jnp.where(here == 0, line, other)
        high = jnp.where(here == 0, other, line)
        return jnp.where(first1, low, high)

    for load in loads:
        load.wait()
    pack_a[...] = pack(src_ref[...].astype(F32))
    pack_b[...] = pack(tgt_ref[...].astype(F32))
    gown_a[...] = own(gf_ref, col)
    gown_b[...] = own(gg_ref, row)
    gath_a[me_a] = pack_a[...]
    gath_b[me_b] = pack_b[...]
    gsl_a[me_a] = gown_a[...]
    gsl_b[me_b] = gown_b[...]
    pl.semaphore_wait(barrier, na + nb - 2)

    for dev, _ in peers_b:
        send(pack_b, gath_b.at[me_b], gsem.at[0], gsem.at[1], dev)
    for dev, _ in peers_a:
        send(pack_a, gath_a.at[me_a], gsem.at[2], gsem.at[3], dev)
    for dev, _ in peers_b:
        send(gown_b, gsl_b.at[me_b], gsem.at[4], gsem.at[5], dev)
    for dev, _ in peers_a:
        send(gown_a, gsl_a.at[me_a], gsem.at[6], gsem.at[7], dev)

    def unpack(gath, out, k):
        one, two = gath[2 * k].astype(F32), gath[2 * k + 1].astype(F32)
        at = slice(k * LANES, (k + 1) * LANES)
        low = jnp.where(first, one, pltpu.roll(two, pts, 1))
        high = jnp.where(first, pltpu.roll(one, pts, 1), two)
        out[0:half, at] = low.astype(BF16)
        out[half:feats, at] = high.astype(BF16)
        return (0.25 * LOG2E) * jnp.sum(low * low + high * high, axis=0, keepdims=True)

    wait_bytes(gath_a.at[pl.ds(0, na - 1)], gsem.at[3])
    sq_i = [unpack(gath_a, x_ref, k) for k in range(ki)]
    wait_bytes(gath_b.at[pl.ds(0, nb - 1)], gsem.at[1])
    sq_j = [unpack(gath_b, y_ref, k) for k in range(kj)]

    def upright(line):
        return jnp.broadcast_to(line, (LANES, LANES)).T

    def lanes(k):
        return slice(k * LANES, (k + 1) * LANES)

    def build(out, tall, sq_tall, wide, sq_wide):
        for k, line in enumerate(sq_tall):
            cross = lax.dot_general(
                tall[0:feats, lanes(k)], wide[0:feats, :], (((0,), (0,)), ((), ())), preferred_element_type=F32
            )
            up = upright(line)
            for s, other in enumerate(sq_wide):
                out[s, lanes(k), :] = (0.5 * LOG2E) * cross[:, lanes(s)] - (up + other)

    STEP = 16

    def steps(k):
        return [slice(h, h + STEP) for h in range(k * LANES, (k + 1) * LANES, STEP)]

    def lse_start(tile, cols):
        for k in range(tile.shape[1] // LANES):
            for at in steps(k):
                vs = [tile[s, at, :] + c for s, c in enumerate(cols)]
                top = tree(vs, jnp.maximum)
                top_ref[at, :] = top
                sum_ref[at, :] = tree([jnp.exp2(v - top) for v in vs], add)

    def lse_finish(i, tile, cols, peers):
        chunks, blocks = tile.shape[0], tile.shape[1] // LANES
        for k in range(blocks):
            tops, sums = [], []
            for at in steps(k):
                if cols is None:
                    vs = [tile[s, at, :] for s in range(chunks)]
                    top = tree(vs, jnp.maximum)
                    total = tree([jnp.exp2(v - top) for v in vs], add)
                else:
                    vs = [tile[chunks - len(cols) + s, at, :] + c for s, c in enumerate(cols)]
                    before = top_ref[at, :]
                    top = jnp.maximum(before, tree(vs, jnp.maximum))
                    total = tree([jnp.exp2(v - top) for v in vs] + [sum_ref[at, :] * jnp.exp2(before - top)], add)
                tops.append(top)
                sums.append(total)
            top = jnp.concatenate(tops, axis=0).T
            total = jnp.concatenate(sums, axis=0).T
            best = jnp.max(top, axis=0, keepdims=True)
            total = jnp.sum(total * jnp.exp2(top - best), axis=0, keepdims=True)
            part, line = k // (blocks // 2), k % (blocks // 2)
            hmine[i, part, line : line + 1, :] = best + jnp.log2(total)
            if line == blocks // 2 - 1:
                for s, (dev, _) in enumerate(peers):
                    send(hmine.at[i, part], hslots.at[i, part, s], hsem.at[i, part], hrsem.at[i, part], dev)

    def post(i, peers):
        for s, (dev, _) in enumerate(peers):
            send(mine.at[i], slots.at[i, s], ssem.at[i], rsem.at[i], dev)

    def arrive(i, peers):
        n = len(peers)
        wait_bytes(slots.at[i, pl.ds(0, n)], rsem.at[i])
        return [mine[i]] + [slots[i, s] for s in range(n)]

    def tree(parts, op):
        while len(parts) > 1:
            parts = [op(parts[t], parts[t + 1]) if t + 1 < len(parts) else parts[t] for t in range(0, len(parts), 2)]
        return parts[0]

    def add(u, v):
        return u + v

    def half_end(i, part, peers):
        n = len(peers)
        wait_bytes(hslots.at[i, part, pl.ds(0, n)], hrsem.at[i, part])
        parts = [hmine[i, part]] + [hslots[i, part, s] for s in range(n)]
        top = tree(parts, jnp.maximum)
        return lines(-(top + jnp.log2(tree([jnp.exp2(p - top) for p in parts], add))))

    def lines(vector):
        return [vector[s : s + 1, :] for s in range(vector.shape[0])]

    build(c_ref, x_ref, sq_i, y_ref, sq_j)
    lse_finish(LR1, c_ref, None, peers_a)
    build(ct_ref, y_ref, sq_j, x_ref, sq_i)
    for i, tile, here, there in (
        (LC1, ct_ref, peers_a, peers_b),
        (LR2, c_ref, peers_b, peers_a),
        (LC2, ct_ref, peers_a, peers_b),
    ):
        one = half_end(i - 1, 0, here)
        lse_start(tile, one)
        two = half_end(i - 1, 1, here)
        lse_finish(i, tile, two, there)
    for k, line in enumerate(one + two):
        fe_ref[lanes(k), :] = upright(line)

    for part in range(2):
        cols = half_end(LC2, part, peers_b)
        at_col = part * len(cols)
        for k in range(ki):
            totals = []
            for at in steps(k):
                up = fe_ref[at, :]
                parts = []
                for s, c in enumerate(cols):
                    e = jnp.exp2((up + c) + c_ref[at_col + s, at, :]).astype(BF16)
                    p_ref[at, lanes(at_col + s)] = e
                    parts.append(e.astype(F32))
                if part:
                    totals.append(tree(parts + [sum_ref[at, :]], add))
                else:
                    sum_ref[at, :] = tree(parts, add)
            if part:
                mine[MASS, k : k + 1, :] = jnp.sum(jnp.concatenate(totals, axis=0).T, axis=0, keepdims=True)
    post(MASS, peers_a)

    def wide_dot(left):
        return jnp.dot(left, p_ref[...], preferred_element_type=F32)

    def tall_dot(left):
        return lax.dot_general(left, p_ref[...], (((1,), (1,)), ((), ())), preferred_element_type=F32)

    xp_ref[...] = wide_dot(x_ref[...])
    for s in range(kj):
        mine[CMASS, s : s + 1, :] = xp_ref[feats : feats + 1, lanes(s)]
    post(CMASS, peers_b)
    yp_ref[...] = tall_dot(y_ref[...])
    wait_bytes(gsl_a.at[pl.ds(0, na - 1)], gsem.at[7])
    wait_bytes(gsl_b.at[pl.ds(0, nb - 1)], gsem.at[5])
    for k in range(ki):
        row_ref[k : k + 1, :] = jnp.where(first1, gsl_a[2 * k], gsl_a[2 * k + 1])
    grad_f = row_ref[0:ki, :]
    for k in range(kj):
        row_ref[k : k + 1, :] = jnp.where(first1, gsl_b[2 * k], gsl_b[2 * k + 1])
    grad_g = row_ref[0:kj, :]

    def load_lhs(vector, width):
        high = vector.astype(BF16).astype(F32)
        rest = vector - high
        mid = rest.astype(BF16).astype(F32)
        low = rest - mid
        for s in range(width // LANES):
            lhs_ref[0:1, lanes(s)] = high[s : s + 1, :]
            lhs_ref[1:2, lanes(s)] = mid[s : s + 1, :]
            lhs_ref[2:3, lanes(s)] = low[s : s + 1, :]
        return lhs_ref[:, 0:width].astype(BF16)

    def keep(i, got):
        got = got[0:1] + got[1:2] + got[2:3]
        for s in range(got.shape[1] // LANES):
            mine[i, s : s + 1, :] = got[:, lanes(s)]

    def row_dot(i, vector):
        keep(i, tall_dot(load_lhs(vector, tj)))
        post(i, peers_a)

    def col_dot(i, vector):
        keep(i, wide_dot(load_lhs(vector, ti)))
        post(i, peers_b)

    row_mass = tree(arrive(MASS, peers_a), add)
    col_dot(PULL, grad_f / row_mass)
    col_mass = tree(arrive(CMASS, peers_b), add)
    residual = grad_g - tree(arrive(PULL, peers_b), add)

    def line_sum(v):
        return jnp.sum(v, axis=0, keepdims=True)

    def extra_post(i, peers):
        for s, (dev, _) in enumerate(peers):
            send(emine.at[i], eslots.at[i, s], essem.at[i], ersem.at[i], dev)

    def extra_arrive(i, peers):
        n = len(peers)
        wait_bytes(eslots.at[i, pl.ds(0, n)], ersem.at[i])
        got = tree([emine[i]] + [eslots[i, s] for s in range(n)], add)
        return jnp.sum(got, axis=1, keepdims=True)

    def spread(points, pulled, part, k):
        grad = 2.0 * (points.astype(F32) * pulled[feats : feats + 1, :] - pulled[0:feats, :])
        low, high = grad[0:half], grad[half:feats]
        part[2 * k] = jnp.where(first, low, pltpu.roll(high, pts, 1)).astype(BF16)
        part[2 * k + 1] = jnp.where(first, pltpu.roll(low, pts, 1), high).astype(BF16)

    def split(out, points, factors):
        rows = points.shape[0]
        for s, factor in enumerate(factors):
            v = points[:, lanes(s)].astype(F32) * factor
            high = v.astype(BF16)
            out[0:rows, lanes(s)] = high
            out[rows : 2 * rows, lanes(s)] = (v - high.astype(F32)).astype(BF16)

    rows = feats + 16

    def tgt_parts(g, us, ws, between):
        split(xu_ref, x_ref, us)
        got = wide_dot(xu_ref[...])
        between()
        for k in range(kj):
            pulled = got[0:rows, lanes(k)] + got[rows:, lanes(k)] + ws[k] * xp_ref[:, lanes(k)]
            spread(y_ref[0:feats, lanes(k)], pulled, part_b.at[g], k)
        for s, (dev, peer) in enumerate(peers_b):
            send(part_b.at[g, peer], rs_b.at[g, s], sgb.at[g], rgb.at[g], dev)

    def src_parts(g, us, pulled_of):
        for k in range(ki):
            spread(x_ref[0:feats, lanes(k)], pulled_of(k) + us[k] * yp_ref[:, lanes(k)], part_a.at[g], k)
        for s, (dev, peer) in enumerate(peers_a):
            send(part_a.at[g, peer], rs_a.at[g, s], sga.at[g], rga.at[g], dev)

    def early_gradients(on_row, on_col, residual, direction):
        us, ws = lines(on_row), lines(on_col)
        for t, vector in enumerate((on_col, residual, direction)):
            split(yw_ref.at[pl.ds(2 * rows * t, 2 * rows)], y_ref, lines(vector))
        got = tall_dot(yw_ref[...])
        for t in range(1, 3):
            at = 2 * rows * t
            yk_ref[t - 1] = got[at : at + rows] + got[at + rows : at + 2 * rows]

        def between():
            src_parts(0, us, lambda k: got[0:rows, lanes(k)] + got[rows : 2 * rows, lanes(k)])

        tgt_parts(0, us, ws, between)

    def late_gradients(on_row, on_col, beta):
        us, ws = lines(on_row), lines(on_col)

        def between():
            src_parts(1, us, lambda k: yk_ref[0, :, lanes(k)] + beta * yk_ref[1, :, lanes(k)])

        tgt_parts(1, us, ws, between)

    dual = pulled_dual = direction = applied = norm = d_c_d = None
    for it in range(CG):
        i_a, i_b = A1 + 2 * it, A1 + 2 * it + 1
        e_a, e_b = 2 * it, 2 * it + 1
        weighted = col_mass * residual
        emine[e_a, 0:1, :] = line_sum(residual * residual)
        emine[e_a, 1:2, :] = line_sum(weighted * residual)
        if it:
            emine[e_a, 2:3, :] = line_sum(weighted * direction)
        extra_post(e_a, peers_a)
        row_dot(i_a, residual)
        if it == CG - 1:
            early_gradients((grad_f - pulled_dual) / row_mass, dual, residual, direction)
        scal = extra_arrive(e_a, peers_a)
        fresh = tree(arrive(i_a, peers_a), add)
        if it:
            beta = scal[0:1] / norm
            direction = residual + beta * direction
            applied = fresh + beta * applied
            d_c_d = scal[1:2] + 2.0 * beta * scal[2:3] + beta * beta * d_c_d
        else:
            direction, applied, d_c_d = residual, fresh, scal[1:2]
        norm = scal[0:1]
        back = applied / row_mass
        emine[e_b, 0:1, :] = line_sum(applied * back)
        extra_post(e_b, peers_b)
        if it == CG - 1:
            late_gradients(-back, direction, beta)
            q_q = extra_arrive(e_b, peers_b)[0:1]
            alpha = norm / ((1.0 + TAU) * d_c_d - q_q)
            continue
        col_dot(i_b, back)
        q_q = extra_arrive(e_b, peers_b)[0:1]
        alpha = norm / ((1.0 + TAU) * d_c_d - q_q)
        dual = alpha * direction if it == 0 else dual + alpha * direction
        pulled_dual = alpha * applied if it == 0 else pulled_dual + alpha * applied
        image = (1.0 + TAU) * col_mass * direction - tree(arrive(i_b, peers_b), add)
        residual = residual - alpha * image

    def collect(g, part, me, slot, n, sem):
        wait_bytes(slot.at[g], sem.at[g])
        return tree([part[g, me].astype(F32)] + [slot[g, s].astype(F32) for s in range(n)], add)

    def store(out, got):
        out[0:half, :] = got[:, 0:pts]
        out[half:feats, :] = got[:, pts:]

    base_a = collect(0, part_a, me_a, rs_a, na - 1, rga)
    base_b = collect(0, part_b, me_b, rs_b, nb - 1, rgb)
    store(osrc_ref, base_a + alpha * collect(1, part_a, me_a, rs_a, na - 1, rga))
    store(otgt_ref, base_b + alpha * collect(1, part_b, me_b, rs_b, nb - 1, rgb))

    wait_bytes(gath_b.at[pl.ds(0, nb - 1)], gsem.at[0])
    wait_bytes(gath_a.at[pl.ds(0, na - 1)], gsem.at[2])
    wait_bytes(gsl_b.at[pl.ds(0, nb - 1)], gsem.at[4])
    wait_bytes(gsl_a.at[pl.ds(0, na - 1)], gsem.at[6])
    for g in range(2):
        wait_bytes(rs_a.at[g], sga.at[g])
        wait_bytes(rs_b.at[g], sgb.at[g])
    over_a = (LR1, LR2, MASS, A1, A1 + 2, A1 + 4)
    for i in range(MASS):
        for part in range(2):
            wait_bytes(hslots.at[i, part, pl.ds(0, len(peers_a if i in over_a else peers_b))], hsem.at[i, part])
    for i in range(MASS, ROUNDS):
        wait_bytes(slots.at[i, pl.ds(0, len(peers_a if i in over_a else peers_b))], ssem.at[i])
    for e in range(2 * CG):
        wait_bytes(eslots.at[e, pl.ds(0, len(peers_a if e % 2 == 0 else peers_b))], essem.at[e])


def hand_over(one_ref, two_ref, first_ref, second_ref):
    first_ref[...] = one_ref[...]
    second_ref[...] = two_ref[...]


def body(sizes, src_points, tgt_points, grad_f, grad_g):
    nx, ny, nz, nc = sizes
    feats, pts = src_points.shape
    na, nb = nx * ny, nz * nc
    ti, tj = na * pts, nb * pts
    ki, kj = ti // LANES, tj // LANES
    n = max(na, nb) - 1
    k = max(ki, kj)
    half = feats // 2
    rows = feats + 16
    vmem = pl.BlockSpec(memory_space=pltpu.VMEM)
    out = jax.ShapeDtypeStruct((feats, pts), F32)
    both = pl.pallas_call(
        functools.partial(kernel, sizes),
        out_shape=(out, out),
        in_specs=[pl.BlockSpec(memory_space=pl.ANY)] * 4,
        out_specs=(vmem, vmem),
        scratch_shapes=[
            pltpu.VMEM((feats, pts), BF16),
            pltpu.VMEM((feats, pts), BF16),
            pltpu.VMEM((grad_f.shape[0] // LANES, LANES), F32),
            pltpu.VMEM((grad_g.shape[0] // LANES, LANES), F32),
            pltpu.VMEM((half, LANES), BF16),
            pltpu.VMEM((half, LANES), BF16),
            pltpu.VMEM((na, half, LANES), BF16),
            pltpu.VMEM((nb, half, LANES), BF16),
            pltpu.VMEM((1, LANES), F32),
            pltpu.VMEM((1, LANES), F32),
            pltpu.VMEM((na, 1, LANES), F32),
            pltpu.VMEM((nb, 1, LANES), F32),
            pltpu.VMEM((rows, ti), BF16),
            pltpu.VMEM((rows, tj), BF16),
            pltpu.VMEM((kj, ti, LANES), F32),
            pltpu.VMEM((ki, tj, LANES), F32),
            pltpu.VMEM((ti, tj), BF16),
            pltpu.VMEM((ti, LANES), F32),
            pltpu.VMEM((8, max(ti, tj)), F32),
            pltpu.VMEM((k, LANES), F32),
            pltpu.VMEM((2 * rows, ti), BF16),
            pltpu.VMEM((6 * rows, tj), BF16),
            pltpu.VMEM((rows, tj), F32),
            pltpu.VMEM((rows, ti), F32),
            pltpu.VMEM((2, rows, ti), F32),
            pltpu.VMEM((ROUNDS, k, LANES), F32),
            pltpu.VMEM((ROUNDS, n, k, LANES), F32),
            pltpu.VMEM((4, 2, k // 2, LANES), F32),
            pltpu.VMEM((4, 2, n, k // 2, LANES), F32),
            pltpu.VMEM((max(ti, tj), LANES), F32),
            pltpu.VMEM((max(ti, tj), LANES), F32),
            pltpu.VMEM((2 * CG, 4, LANES), F32),
            pltpu.VMEM((2 * CG, n, 4, LANES), F32),
            pltpu.VMEM((2, na, half, LANES), BF16),
            pltpu.VMEM((2, nb, half, LANES), BF16),
            pltpu.VMEM((2, na - 1, half, LANES), BF16),
            pltpu.VMEM((2, nb - 1, half, LANES), BF16),
            pltpu.SemaphoreType.DMA((4,)),
            pltpu.SemaphoreType.DMA((8,)),
            pltpu.SemaphoreType.DMA((4, 2)),
            pltpu.SemaphoreType.DMA((4, 2)),
            pltpu.SemaphoreType.DMA((ROUNDS,)),
            pltpu.SemaphoreType.DMA((ROUNDS,)),
            pltpu.SemaphoreType.DMA((2 * CG,)),
            pltpu.SemaphoreType.DMA((2 * CG,)),
            pltpu.SemaphoreType.DMA((2,)),
            pltpu.SemaphoreType.DMA((2,)),
            pltpu.SemaphoreType.DMA((2,)),
            pltpu.SemaphoreType.DMA((2,)),
        ],
        compiler_params=pltpu.CompilerParams(
            collective_id=0, has_side_effects=True, vmem_limit_bytes=56 * 1024 * 1024
        ),
        name="transport",
    )(src_points, tgt_points, grad_f.reshape(-1, LANES), grad_g.reshape(-1, LANES))
    return pl.pallas_call(
        hand_over, out_shape=(out, out), in_specs=[vmem] * 2, out_specs=(vmem, vmem), name="hand_over"
    )(*both)


def solution(mesh):
    rows, cols = mesh.shape["row"], mesh.shape["col"]
    sizes = (4, cols // 4, rows // 2, 2)
    in_specs = (P(None, ("row", "col")), P(None, ("col", "row")), P("row"), P("col"))
    out_specs = (P(None, ("row", "col")), P(None, ("col", "row")))
    return jax.shard_map(
        functools.partial(body, sizes), mesh=mesh, in_specs=in_specs, out_specs=out_specs, check_vma=False
    )
```

```python
import functools
import math

import jax
import jax.numpy as jnp
from jax import lax
from jax.experimental import pallas as pl
from jax.experimental.pallas import tpu as pltpu
from jax.sharding import PartitionSpec as P

CG = 3
TAU = 0.1
LOG2E = math.log2(math.e)
LANES = 128
MESH = pl.DeviceIdType.MESH
F32 = jnp.float32
BF16 = jnp.bfloat16

LR1, LC1, LR2, LC2, MASS, PULL, CMASS, A1 = range(8)
ROUNDS = 12


def ring(d, n):
    return min(d % n, n - d % n)


def kernel(
    sizes, src_hbm, tgt_hbm, gf_hbm, gg_hbm, osrc_ref, otgt_ref,
    src_ref, tgt_ref, gf_ref, gg_ref,
    pack_a, pack_b, gath_a, gath_b, gown_a, gown_b, gsl_a, gsl_b,
    x_ref, y_ref, c_ref, ct_ref, p_ref, pt_ref, fe_ref, lhs_ref, row_ref, xu_ref, yw_ref, xp_ref, yp_ref, yk_ref,
    mine, slots, hmine, hslots, top_ref, sum_ref, emine, eslots, part_a, part_b, rs_a, rs_b,
    isem, gsem, hsem, hrsem, ssem, rsem, essem, ersem, sga, rga, sgb, rgb,
):
    nx, ny, nz, nc = sizes
    na, nb = nx * ny, nz * nc
    row, col = lax.axis_index("row"), lax.axis_index("col")
    z, x_lo = lax.div(row, 2), lax.rem(row, 2)
    x_hi, y, core = lax.div(col, 2 * ny), lax.rem(lax.div(col, 2), ny), lax.rem(col, 2)
    x = x_hi * 2 + x_lo
    me_a, me_b = x * ny + y, z * nc + core
    feats, pts = src_ref.shape
    half = feats // 2
    ti, tj = na * pts, nb * pts
    ki, kj = ti // LANES, tj // LANES

    offs_a = [(i, j) for i in range(nx) for j in range(ny) if i or j]
    offs_a.sort(key=lambda o: -(ring(o[0], nx) + ring(o[1], ny)))
    offs_b = [(i, j) for i in range(nz) for j in range(nc) if i or j]
    offs_b.sort(key=lambda o: -(ring(o[0], nz) + 0.1 * o[1]))
    peers_a, peers_b = [], []
    xs = [lax.rem(x + d, nx) for d in range(nx)]
    xs = [(z * 2 + lax.rem(p, 2), lax.div(p, 2) * (2 * ny) + core, p * ny) for p in xs]
    ys = [lax.rem(y + d, ny) for d in range(ny)]
    zs = [lax.rem(z + d, nz) for d in range(nz)]
    zs = [(p * 2 + x_lo, p * nc) for p in zs]
    cs = [(col - core + p, p) for p in (core, 1 - core)]
    for dx, dy in offs_a:
        peers_a.append(((xs[dx][0], xs[dx][1] + ys[dy] * 2), xs[dx][2] + ys[dy]))
    for dz, dc in offs_b:
        peers_b.append(((zs[dz][0], cs[dc][0]), zs[dz][1] + cs[dc][1]))

    def send(src, dst, s_sem, r_sem, dev):
        pltpu.make_async_remote_copy(
            src_ref=src, dst_ref=dst, send_sem=s_sem, recv_sem=r_sem, device_id=dev, device_id_type=MESH
        ).start()

    def wait_bytes(ref, sem):
        pltpu.make_async_copy(ref, ref, sem).wait()

    barrier = pltpu.get_barrier_semaphore()
    for dev, _ in peers_b + peers_a:
        pl.semaphore_signal(barrier, inc=1, device_id=dev, device_id_type=MESH)
    loads = [
        pltpu.make_async_copy(here, there, isem.at[n])
        for n, (here, there) in enumerate(
            ((src_hbm, src_ref), (tgt_hbm, tgt_ref), (gf_hbm, gf_ref), (gg_hbm, gg_ref))
        )
    ]
    for load in loads:
        load.start()

    first = lax.broadcasted_iota(jnp.int32, (half, LANES), 1) < pts
    first1 = lax.broadcasted_iota(jnp.int32, (1, LANES), 1) < pts
    lhs_ref[...] = jnp.zeros_like(lhs_ref)
    emine[...] = jnp.zeros_like(emine)
    for ref in (x_ref, y_ref):
        pad = (ref.shape[0] - feats, ref.shape[1])
        ref[feats:, :] = (lax.broadcasted_iota(jnp.int32, pad, 0) == 0).astype(F32).astype(BF16)

    def pack(block):
        return jnp.concatenate([block[:half], block[half:]], axis=1).astype(BF16)

    def own(ref, at):
        line = ref[pl.ds(lax.div(at, 2), 1), :]
        other = pltpu.roll(line, pts, 1)
        here = lax.rem(at, 2)
        low = jnp.where(here == 0, line, other)
        high = jnp.where(here == 0, other, line)
        return jnp.where(first1, low, high)

    for load in loads:
        load.wait()
    pack_a[...] = pack(src_ref[...].astype(F32))
    pack_b[...] = pack(tgt_ref[...].astype(F32))
    gown_a[...] = own(gf_ref, col)
    gown_b[...] = own(gg_ref, row)
    gath_a[me_a] = pack_a[...]
    gath_b[me_b] = pack_b[...]
    gsl_a[me_a] = gown_a[...]
    gsl_b[me_b] = gown_b[...]
    pl.semaphore_wait(barrier, na + nb - 2)

    for dev, _ in peers_b:
        send(pack_b, gath_b.at[me_b], gsem.at[0], gsem.at[1], dev)
    for dev, _ in peers_a:
        send(pack_a, gath_a.at[me_a], gsem.at[2], gsem.at[3], dev)
    for dev, _ in peers_b:
        send(gown_b, gsl_b.at[me_b], gsem.at[4], gsem.at[5], dev)
    for dev, _ in peers_a:
        send(gown_a, gsl_a.at[me_a], gsem.at[6], gsem.at[7], dev)

    def unpack(gath, out, k):
        one, two = gath[2 * k].astype(F32), gath[2 * k + 1].astype(F32)
        at = slice(k * LANES, (k + 1) * LANES)
        low = jnp.where(first, one, pltpu.roll(two, pts, 1))
        high = jnp.where(first, pltpu.roll(one, pts, 1), two)
        out[0:half, at] = low.astype(BF16)
        out[half:feats, at] = high.astype(BF16)
        return (0.25 * LOG2E) * jnp.sum(low * low + high * high, axis=0, keepdims=True)

    wait_bytes(gath_a.at[pl.ds(0, na - 1)], gsem.at[3])
    sq_i = [unpack(gath_a, x_ref, k) for k in range(ki)]
    wait_bytes(gath_b.at[pl.ds(0, nb - 1)], gsem.at[1])
    sq_j = [unpack(gath_b, y_ref, k) for k in range(kj)]

    def upright(line):
        return jnp.broadcast_to(line, (LANES, LANES)).T

    def lanes(k):
        return slice(k * LANES, (k + 1) * LANES)

    def build(out, tall, sq_tall, wide, sq_wide):
        for k, line in enumerate(sq_tall):
            cross = lax.dot_general(
                tall[0:feats, lanes(k)], wide[0:feats, :], (((0,), (0,)), ((), ())), preferred_element_type=F32
            )
            up = upright(line)
            for s, other in enumerate(sq_wide):
                out[s, lanes(k), :] = (0.5 * LOG2E) * cross[:, lanes(s)] - (up + other)

    STEP = 16

    def steps(k):
        return [slice(h, h + STEP) for h in range(k * LANES, (k + 1) * LANES, STEP)]

    def lse_start(tile, cols):
        for k in range(tile.shape[1] // LANES):
            for at in steps(k):
                vs = [tile[s, at, :] + c for s, c in enumerate(cols)]
                top = tree(vs, jnp.maximum)
                top_ref[at, :] = top
                sum_ref[at, :] = tree([jnp.exp2(v - top) for v in vs], add)

    def lse_finish(i, tile, cols, peers):
        chunks, blocks = tile.shape[0], tile.shape[1] // LANES
        for k in range(blocks):
            tops, sums = [], []
            for at in steps(k):
                if cols is None:
                    vs = [tile[s, at, :] for s in range(chunks)]
                    top = tree(vs, jnp.maximum)
                    total = tree([jnp.exp2(v - top) for v in vs], add)
                else:
                    vs = [tile[chunks - len(cols) + s, at, :] + c for s, c in enumerate(cols)]
                    before = top_ref[at, :]
                    top = jnp.maximum(before, tree(vs, jnp.maximum))
                    total = tree([jnp.exp2(v - top) for v in vs] + [sum_ref[at, :] * jnp.exp2(before - top)], add)
                tops.append(top)
                sums.append(total)
            top = jnp.concatenate(tops, axis=0).T
            total = jnp.concatenate(sums, axis=0).T
            best = jnp.max(top, axis=0, keepdims=True)
            total = jnp.sum(total * jnp.exp2(top - best), axis=0, keepdims=True)
            part, line = k // (blocks // 2), k % (blocks // 2)
            hmine[i, part, line : line + 1, :] = best + jnp.log2(total)
            if line == blocks // 2 - 1:
                for s, (dev, _) in enumerate(peers):
                    send(hmine.at[i, part], hslots.at[i, part, s], hsem.at[i, part], hrsem.at[i, part], dev)

    def post(i, peers):
        for s, (dev, _) in enumerate(peers):
            send(mine.at[i], slots.at[i, s], ssem.at[i], rsem.at[i], dev)

    def arrive(i, peers):
        n = len(peers)
        wait_bytes(slots.at[i, pl.ds(0, n)], rsem.at[i])
        return [mine[i]] + [slots[i, s] for s in range(n)]

    def tree(parts, op):
        while len(parts) > 1:
            parts = [op(parts[t], parts[t + 1]) if t + 1 < len(parts) else parts[t] for t in range(0, len(parts), 2)]
        return parts[0]

    def add(u, v):
        return u + v

    def half_end(i, part, peers):
        n = len(peers)
        wait_bytes(hslots.at[i, part, pl.ds(0, n)], hrsem.at[i, part])
        parts = [hmine[i, part]] + [hslots[i, part, s] for s in range(n)]
        top = tree(parts, jnp.maximum)
        return lines(-(top + jnp.log2(tree([jnp.exp2(p - top) for p in parts], add))))

    def lines(vector):
        return [vector[s : s + 1, :] for s in range(vector.shape[0])]

    build(c_ref, x_ref, sq_i, y_ref, sq_j)
    lse_finish(LR1, c_ref, None, peers_a)
    build(ct_ref, y_ref, sq_j, x_ref, sq_i)
    for i, tile, here, there in (
        (LC1, ct_ref, peers_a, peers_b),
        (LR2, c_ref, peers_b, peers_a),
        (LC2, ct_ref, peers_a, peers_b),
    ):
        one = half_end(i - 1, 0, here)
        lse_start(tile, one)
        two = half_end(i - 1, 1, here)
        lse_finish(i, tile, two, there)
    for k, line in enumerate(one + two):
        fe_ref[lanes(k), :] = upright(line)

    for part in range(2):
        cols = half_end(LC2, part, peers_b)
        at_col = part * len(cols)
        for k in range(ki):
            totals = []
            for at in steps(k):
                up = fe_ref[at, :]
                parts = []
                for s, c in enumerate(cols):
                    e = jnp.exp2((up + c) + c_ref[at_col + s, at, :]).astype(BF16)
                    p_ref[at, lanes(at_col + s)] = e
                    parts.append(e.astype(F32))
                if part:
                    totals.append(tree(parts + [sum_ref[at, :]], add))
                else:
                    sum_ref[at, :] = tree(parts, add)
            if part:
                mine[MASS, k : k + 1, :] = jnp.sum(jnp.concatenate(totals, axis=0).T, axis=0, keepdims=True)
    post(MASS, peers_a)

    def wide_dot(left):
        return jnp.dot(left, p_ref[...], preferred_element_type=F32)

    def tall_dot(left):
        return jnp.dot(left, pt_ref[...], preferred_element_type=F32)

    xp_ref[...] = wide_dot(x_ref[...])
    for s in range(kj):
        mine[CMASS, s : s + 1, :] = xp_ref[feats : feats + 1, lanes(s)]
    post(CMASS, peers_b)
    for k in range(ki):
        for s in range(kj):
            pt_ref[lanes(s), lanes(k)] = p_ref[lanes(k), lanes(s)].T
    wait_bytes(gsl_a.at[pl.ds(0, na - 1)], gsem.at[7])
    wait_bytes(gsl_b.at[pl.ds(0, nb - 1)], gsem.at[5])
    for k in range(ki):
        row_ref[k : k + 1, :] = jnp.where(first1, gsl_a[2 * k], gsl_a[2 * k + 1])
    grad_f = row_ref[0:ki, :]
    for k in range(kj):
        row_ref[k : k + 1, :] = jnp.where(first1, gsl_b[2 * k], gsl_b[2 * k + 1])
    grad_g = row_ref[0:kj, :]

    def load_lhs(vector, width):
        high = vector.astype(BF16).astype(F32)
        rest = vector - high
        mid = rest.astype(BF16).astype(F32)
        low = rest - mid
        for s in range(width // LANES):
            lhs_ref[0:1, lanes(s)] = high[s : s + 1, :]
            lhs_ref[1:2, lanes(s)] = mid[s : s + 1, :]
            lhs_ref[2:3, lanes(s)] = low[s : s + 1, :]
        return lhs_ref[:, 0:width].astype(BF16)

    def keep(i, got):
        got = got[0:1] + got[1:2] + got[2:3]
        for s in range(got.shape[1] // LANES):
            mine[i, s : s + 1, :] = got[:, lanes(s)]

    def row_dot(i, vector):
        keep(i, tall_dot(load_lhs(vector, tj)))
        post(i, peers_a)

    def col_dot(i, vector):
        keep(i, wide_dot(load_lhs(vector, ti)))
        post(i, peers_b)

    row_mass = tree(arrive(MASS, peers_a), add)
    col_dot(PULL, grad_f / row_mass)
    yp_ref[...] = tall_dot(y_ref[...])
    col_mass = tree(arrive(CMASS, peers_b), add)
    residual = grad_g - tree(arrive(PULL, peers_b), add)

    def line_sum(v):
        return jnp.sum(v, axis=0, keepdims=True)

    def extra_post(i, peers):
        for s, (dev, _) in enumerate(peers):
            send(emine.at[i], eslots.at[i, s], essem.at[i], ersem.at[i], dev)

    def extra_arrive(i, peers):
        n = len(peers)
        wait_bytes(eslots.at[i, pl.ds(0, n)], ersem.at[i])
        got = tree([emine[i]] + [eslots[i, s] for s in range(n)], add)
        return jnp.sum(got, axis=1, keepdims=True)

    def spread(points, pulled, part, k):
        grad = 2.0 * (points.astype(F32) * pulled[feats : feats + 1, :] - pulled[0:feats, :])
        low, high = grad[0:half], grad[half:feats]
        part[2 * k] = jnp.where(first, low, pltpu.roll(high, pts, 1)).astype(BF16)
        part[2 * k + 1] = jnp.where(first, pltpu.roll(low, pts, 1), high).astype(BF16)

    def split(out, points, factors):
        rows = points.shape[0]
        for s, factor in enumerate(factors):
            v = points[:, lanes(s)].astype(F32) * factor
            high = v.astype(BF16)
            out[0:rows, lanes(s)] = high
            out[rows : 2 * rows, lanes(s)] = (v - high.astype(F32)).astype(BF16)

    rows = feats + 16

    def tgt_parts(g, us, ws, between):
        split(xu_ref, x_ref, us)
        got = wide_dot(xu_ref[...])
        between()
        for k in range(kj):
            pulled = got[0:rows, lanes(k)] + got[rows:, lanes(k)] + ws[k] * xp_ref[:, lanes(k)]
            spread(y_ref[0:feats, lanes(k)], pulled, part_b.at[g], k)
        for s, (dev, peer) in enumerate(peers_b):
            send(part_b.at[g, peer], rs_b.at[g, s], sgb.at[g], rgb.at[g], dev)

    def src_parts(g, us, pulled_of):
        for k in range(ki):
            spread(x_ref[0:feats, lanes(k)], pulled_of(k) + us[k] * yp_ref[:, lanes(k)], part_a.at[g], k)
        for s, (dev, peer) in enumerate(peers_a):
            send(part_a.at[g, peer], rs_a.at[g, s], sga.at[g], rga.at[g], dev)

    def early_gradients(on_row, on_col, residual, direction):
        us, ws = lines(on_row), lines(on_col)
        for t, vector in enumerate((on_col, residual, direction)):
            split(yw_ref.at[pl.ds(2 * rows * t, 2 * rows)], y_ref, lines(vector))
        got = tall_dot(yw_ref[...])
        for t in range(1, 3):
            at = 2 * rows * t
            yk_ref[t - 1] = got[at : at + rows] + got[at + rows : at + 2 * rows]

        def between():
            src_parts(0, us, lambda k: got[0:rows, lanes(k)] + got[rows : 2 * rows, lanes(k)])

        tgt_parts(0, us, ws, between)

    def late_gradients(on_row, on_col, beta):
        us, ws = lines(on_row), lines(on_col)

        def between():
            src_parts(1, us, lambda k: yk_ref[0, :, lanes(k)] + beta * yk_ref[1, :, lanes(k)])

        tgt_parts(1, us, ws, between)

    dual = pulled_dual = direction = applied = norm = d_c_d = None
    for it in range(CG):
        i_a, i_b = A1 + 2 * it, A1 + 2 * it + 1
        e_a, e_b = 2 * it, 2 * it + 1
        weighted = col_mass * residual
        emine[e_a, 0:1, :] = line_sum(residual * residual)
        emine[e_a, 1:2, :] = line_sum(weighted * residual)
        if it:
            emine[e_a, 2:3, :] = line_sum(weighted * direction)
        extra_post(e_a, peers_a)
        row_dot(i_a, residual)
        if it == CG - 1:
            early_gradients((grad_f - pulled_dual) / row_mass, dual, residual, direction)
        scal = extra_arrive(e_a, peers_a)
        fresh = tree(arrive(i_a, peers_a), add)
        if it:
            beta = scal[0:1] / norm
            direction = residual + beta * direction
            applied = fresh + beta * applied
            d_c_d = scal[1:2] + 2.0 * beta * scal[2:3] + beta * beta * d_c_d
        else:
            direction, applied, d_c_d = residual, fresh, scal[1:2]
        norm = scal[0:1]
        back = applied / row_mass
        emine[e_b, 0:1, :] = line_sum(applied * back)
        extra_post(e_b, peers_b)
        if it == CG - 1:
            late_gradients(-back, direction, beta)
            q_q = extra_arrive(e_b, peers_b)[0:1]
            alpha = norm / ((1.0 + TAU) * d_c_d - q_q)
            continue
        col_dot(i_b, back)
        q_q = extra_arrive(e_b, peers_b)[0:1]
        alpha = norm / ((1.0 + TAU) * d_c_d - q_q)
        dual = alpha * direction if it == 0 else dual + alpha * direction
        pulled_dual = alpha * applied if it == 0 else pulled_dual + alpha * applied
        image = (1.0 + TAU) * col_mass * direction - tree(arrive(i_b, peers_b), add)
        residual = residual - alpha * image

    def collect(g, part, me, slot, n, sem):
        wait_bytes(slot.at[g], sem.at[g])
        return tree([part[g, me].astype(F32)] + [slot[g, s].astype(F32) for s in range(n)], add)

    def store(out, got):
        out[0:half, :] = got[:, 0:pts]
        out[half:feats, :] = got[:, pts:]

    base_a = collect(0, part_a, me_a, rs_a, na - 1, rga)
    base_b = collect(0, part_b, me_b, rs_b, nb - 1, rgb)
    store(osrc_ref, base_a + alpha * collect(1, part_a, me_a, rs_a, na - 1, rga))
    store(otgt_ref, base_b + alpha * collect(1, part_b, me_b, rs_b, nb - 1, rgb))

    wait_bytes(gath_b.at[pl.ds(0, nb - 1)], gsem.at[0])
    wait_bytes(gath_a.at[pl.ds(0, na - 1)], gsem.at[2])
    wait_bytes(gsl_b.at[pl.ds(0, nb - 1)], gsem.at[4])
    wait_bytes(gsl_a.at[pl.ds(0, na - 1)], gsem.at[6])
    for g in range(2):
        wait_bytes(rs_a.at[g], sga.at[g])
        wait_bytes(rs_b.at[g], sgb.at[g])
    over_a = (LR1, LR2, MASS, A1, A1 + 2, A1 + 4)
    for i in range(MASS):
        for part in range(2):
            wait_bytes(hslots.at[i, part, pl.ds(0, len(peers_a if i in over_a else peers_b))], hsem.at[i, part])
    for i in range(MASS, ROUNDS):
        wait_bytes(slots.at[i, pl.ds(0, len(peers_a if i in over_a else peers_b))], ssem.at[i])
    for e in range(2 * CG):
        wait_bytes(eslots.at[e, pl.ds(0, len(peers_a if e % 2 == 0 else peers_b))], essem.at[e])


def hand_over(one_ref, two_ref, first_ref, second_ref):
    first_ref[...] = one_ref[...]
    second_ref[...] = two_ref[...]


def body(sizes, src_points, tgt_points, grad_f, grad_g):
    nx, ny, nz, nc = sizes
    feats, pts = src_points.shape
    na, nb = nx * ny, nz * nc
    ti, tj = na * pts, nb * pts
    ki, kj = ti // LANES, tj // LANES
    n = max(na, nb) - 1
    k = max(ki, kj)
    half = feats // 2
    rows = feats + 16
    vmem = pl.BlockSpec(memory_space=pltpu.VMEM)
    out = jax.ShapeDtypeStruct((feats, pts), F32)
    both = pl.pallas_call(
        functools.partial(kernel, sizes),
        out_shape=(out, out),
        in_specs=[pl.BlockSpec(memory_space=pl.ANY)] * 4,
        out_specs=(vmem, vmem),
        scratch_shapes=[
            pltpu.VMEM((feats, pts), BF16),
            pltpu.VMEM((feats, pts), BF16),
            pltpu.VMEM((grad_f.shape[0] // LANES, LANES), F32),
            pltpu.VMEM((grad_g.shape[0] // LANES, LANES), F32),
            pltpu.VMEM((half, LANES), BF16),
            pltpu.VMEM((half, LANES), BF16),
            pltpu.VMEM((na, half, LANES), BF16),
            pltpu.VMEM((nb, half, LANES), BF16),
            pltpu.VMEM((1, LANES), F32),
            pltpu.VMEM((1, LANES), F32),
            pltpu.VMEM((na, 1, LANES), F32),
            pltpu.VMEM((nb, 1, LANES), F32),
            pltpu.VMEM((rows, ti), BF16),
            pltpu.VMEM((rows, tj), BF16),
            pltpu.VMEM((kj, ti, LANES), F32),
            pltpu.VMEM((ki, tj, LANES), F32),
            pltpu.VMEM((ti, tj), BF16),
            pltpu.VMEM((tj, ti), BF16),
            pltpu.VMEM((ti, LANES), F32),
            pltpu.VMEM((8, max(ti, tj)), F32),
            pltpu.VMEM((k, LANES), F32),
            pltpu.VMEM((2 * rows, ti), BF16),
            pltpu.VMEM((6 * rows, tj), BF16),
            pltpu.VMEM((rows, tj), F32),
            pltpu.VMEM((rows, ti), F32),
            pltpu.VMEM((2, rows, ti), F32),
            pltpu.VMEM((ROUNDS, k, LANES), F32),
            pltpu.VMEM((ROUNDS, n, k, LANES), F32),
            pltpu.VMEM((4, 2, k // 2, LANES), F32),
            pltpu.VMEM((4, 2, n, k // 2, LANES), F32),
            pltpu.VMEM((max(ti, tj), LANES), F32),
            pltpu.VMEM((max(ti, tj), LANES), F32),
            pltpu.VMEM((2 * CG, 4, LANES), F32),
            pltpu.VMEM((2 * CG, n, 4, LANES), F32),
            pltpu.VMEM((2, na, half, LANES), BF16),
            pltpu.VMEM((2, nb, half, LANES), BF16),
            pltpu.VMEM((2, na - 1, half, LANES), BF16),
            pltpu.VMEM((2, nb - 1, half, LANES), BF16),
            pltpu.SemaphoreType.DMA((4,)),
            pltpu.SemaphoreType.DMA((8,)),
            pltpu.SemaphoreType.DMA((4, 2)),
            pltpu.SemaphoreType.DMA((4, 2)),
            pltpu.SemaphoreType.DMA((ROUNDS,)),
            pltpu.SemaphoreType.DMA((ROUNDS,)),
            pltpu.SemaphoreType.DMA((2 * CG,)),
            pltpu.SemaphoreType.DMA((2 * CG,)),
            pltpu.SemaphoreType.DMA((2,)),
            pltpu.SemaphoreType.DMA((2,)),
            pltpu.SemaphoreType.DMA((2,)),
            pltpu.SemaphoreType.DMA((2,)),
        ],
        compiler_params=pltpu.CompilerParams(
            collective_id=0, has_side_effects=True, vmem_limit_bytes=56 * 1024 * 1024
        ),
        name="transport",
    )(src_points, tgt_points, grad_f.reshape(-1, LANES), grad_g.reshape(-1, LANES))
    return pl.pallas_call(
        hand_over, out_shape=(out, out), in_specs=[vmem] * 2, out_specs=(vmem, vmem), name="hand_over"
    )(*both)


def solution(mesh):
    rows, cols = mesh.shape["row"], mesh.shape["col"]
    sizes = (4, cols // 4, rows // 2, 2)
    in_specs = (P(None, ("row", "col")), P(None, ("col", "row")), P("row"), P("col"))
    out_specs = (P(None, ("row", "col")), P(None, ("col", "row")))
    return jax.shard_map(
        functools.partial(body, sizes), mesh=mesh, in_specs=in_specs, out_specs=out_specs, check_vma=False
    )
```

```python
import functools
import math

import jax
import jax.numpy as jnp
from jax import lax
from jax.experimental import pallas as pl
from jax.experimental.pallas import tpu as pltpu
from jax.sharding import PartitionSpec as P

CG = 3
TAU = 0.1
LOG2E = math.log2(math.e)
LANES = 128
MESH = pl.DeviceIdType.MESH
F32 = jnp.float32
BF16 = jnp.bfloat16

LR1, LC1, LR2, LC2, MASS, PULL, CMASS = range(7)
ROUNDS = 7


def ring(d, n):
    return min(d % n, n - d % n)


def kernel(
    sizes, src_hbm, tgt_hbm, gf_hbm, gg_hbm, osrc_ref, otgt_ref,
    src_ref, tgt_ref, gf_ref, gg_ref,
    pack_a, pack_b, gath_a, gath_b, gown_a, gown_b, gsl_a, gsl_b,
    x_ref, y_ref, c_ref, ct_ref, p_ref, pt_ref, fe_ref, lhs_ref, row_ref, xu_ref, yw_ref, xp_ref, yp_ref, yk_ref,
    mine, slots, hmine, hslots, top_ref, sum_ref, cmine, cslots, emine, eslots, part_a, part_b, rs_a, rs_b,
    isem, gsem, hsem, hrsem, csem, crsem, ssem, rsem, essem, ersem, sga, rga, sgb, rgb,
):
    nx, ny, nz, nc = sizes
    na, nb = nx * ny, nz * nc
    row, col = lax.axis_index("row"), lax.axis_index("col")
    z, x_lo = lax.div(row, 2), lax.rem(row, 2)
    x_hi, y, core = lax.div(col, 2 * ny), lax.rem(lax.div(col, 2), ny), lax.rem(col, 2)
    x = x_hi * 2 + x_lo
    me_a, me_b = x * ny + y, z * nc + core
    feats, pts = src_ref.shape
    half = feats // 2
    ti, tj = na * pts, nb * pts
    ki, kj = ti // LANES, tj // LANES

    offs_a = [(i, j) for i in range(nx) for j in range(ny) if i or j]
    offs_a.sort(key=lambda o: -(ring(o[0], nx) + ring(o[1], ny)))
    offs_b = [(i, j) for i in range(nz) for j in range(nc) if i or j]
    offs_b.sort(key=lambda o: -(ring(o[0], nz) + 0.1 * o[1]))
    peers_a, peers_b = [], []
    xs = [lax.rem(x + d, nx) for d in range(nx)]
    xs = [(z * 2 + lax.rem(p, 2), lax.div(p, 2) * (2 * ny) + core, p * ny) for p in xs]
    ys = [lax.rem(y + d, ny) for d in range(ny)]
    zs = [lax.rem(z + d, nz) for d in range(nz)]
    zs = [(p * 2 + x_lo, p * nc) for p in zs]
    cs = [(col - core + p, p) for p in (core, 1 - core)]
    for dx, dy in offs_a:
        peers_a.append(((xs[dx][0], xs[dx][1] + ys[dy] * 2), xs[dx][2] + ys[dy]))
    for dz, dc in offs_b:
        peers_b.append(((zs[dz][0], cs[dc][0]), zs[dz][1] + cs[dc][1]))

    def send(src, dst, s_sem, r_sem, dev):
        pltpu.make_async_remote_copy(
            src_ref=src, dst_ref=dst, send_sem=s_sem, recv_sem=r_sem, device_id=dev, device_id_type=MESH
        ).start()

    def wait_bytes(ref, sem):
        pltpu.make_async_copy(ref, ref, sem).wait()

    barrier = pltpu.get_barrier_semaphore()
    for dev, _ in peers_b + peers_a:
        pl.semaphore_signal(barrier, inc=1, device_id=dev, device_id_type=MESH)
    loads = [
        pltpu.make_async_copy(here, there, isem.at[n])
        for n, (here, there) in enumerate(
            ((src_hbm, src_ref), (tgt_hbm, tgt_ref), (gf_hbm, gf_ref), (gg_hbm, gg_ref))
        )
    ]
    for load in loads:
        load.start()

    first = lax.broadcasted_iota(jnp.int32, (half, LANES), 1) < pts
    first1 = lax.broadcasted_iota(jnp.int32, (1, LANES), 1) < pts
    lhs_ref[...] = jnp.zeros_like(lhs_ref)
    emine[...] = jnp.zeros_like(emine)
    cmine[...] = jnp.zeros_like(cmine)
    for ref in (x_ref, y_ref):
        pad = (ref.shape[0] - feats, ref.shape[1])
        ref[feats:, :] = (lax.broadcasted_iota(jnp.int32, pad, 0) == 0).astype(F32).astype(BF16)

    def pack(block):
        return jnp.concatenate([block[:half], block[half:]], axis=1).astype(BF16)

    def own(ref, at):
        line = ref[pl.ds(lax.div(at, 2), 1), :]
        other = pltpu.roll(line, pts, 1)
        here = lax.rem(at, 2)
        low = jnp.where(here == 0, line, other)
        high = jnp.where(here == 0, other, line)
        return jnp.where(first1, low, high)

    for load in loads:
        load.wait()
    pack_a[...] = pack(src_ref[...].astype(F32))
    pack_b[...] = pack(tgt_ref[...].astype(F32))
    gown_a[...] = own(gf_ref, col)
    gown_b[...] = own(gg_ref, row)
    gath_a[me_a] = pack_a[...]
    gath_b[me_b] = pack_b[...]
    gsl_a[me_a] = gown_a[...]
    gsl_b[me_b] = gown_b[...]
    pl.semaphore_wait(barrier, na + nb - 2)

    for dev, _ in peers_b:
        send(pack_b, gath_b.at[me_b], gsem.at[0], gsem.at[1], dev)
    for dev, _ in peers_a:
        send(pack_a, gath_a.at[me_a], gsem.at[2], gsem.at[3], dev)
    for dev, _ in peers_b:
        send(gown_b, gsl_b.at[me_b], gsem.at[4], gsem.at[5], dev)
    for dev, _ in peers_a:
        send(gown_a, gsl_a.at[me_a], gsem.at[6], gsem.at[7], dev)

    def unpack(gath, out, k):
        one, two = gath[2 * k].astype(F32), gath[2 * k + 1].astype(F32)
        at = slice(k * LANES, (k + 1) * LANES)
        low = jnp.where(first, one, pltpu.roll(two, pts, 1))
        high = jnp.where(first, pltpu.roll(one, pts, 1), two)
        out[0:half, at] = low.astype(BF16)
        out[half:feats, at] = high.astype(BF16)
        return (0.25 * LOG2E) * jnp.sum(low * low + high * high, axis=0, keepdims=True)

    wait_bytes(gath_a.at[pl.ds(0, na - 1)], gsem.at[3])
    sq_i = [unpack(gath_a, x_ref, k) for k in range(ki)]
    wait_bytes(gath_b.at[pl.ds(0, nb - 1)], gsem.at[1])
    sq_j = [unpack(gath_b, y_ref, k) for k in range(kj)]

    def upright(line):
        return jnp.broadcast_to(line, (LANES, LANES)).T

    def lanes(k):
        return slice(k * LANES, (k + 1) * LANES)

    def build(out, tall, sq_tall, wide, sq_wide):
        for k, line in enumerate(sq_tall):
            cross = lax.dot_general(
                tall[0:feats, lanes(k)], wide[0:feats, :], (((0,), (0,)), ((), ())), preferred_element_type=F32
            )
            up = upright(line)
            for s, other in enumerate(sq_wide):
                out[s, lanes(k), :] = (0.5 * LOG2E) * cross[:, lanes(s)] - (up + other)

    STEP = 16

    def steps(k):
        return [slice(h, h + STEP) for h in range(k * LANES, (k + 1) * LANES, STEP)]

    def lse_start(tile, cols):
        for k in range(tile.shape[1] // LANES):
            for at in steps(k):
                vs = [tile[s, at, :] + c for s, c in enumerate(cols)]
                top = tree(vs, jnp.maximum)
                top_ref[at, :] = top
                sum_ref[at, :] = tree([jnp.exp2(v - top) for v in vs], add)

    def lse_finish(i, tile, cols, peers):
        chunks, blocks = tile.shape[0], tile.shape[1] // LANES
        for k in range(blocks):
            tops, sums = [], []
            for at in steps(k):
                if cols is None:
                    vs = [tile[s, at, :] for s in range(chunks)]
                    top = tree(vs, jnp.maximum)
                    total = tree([jnp.exp2(v - top) for v in vs], add)
                else:
                    vs = [tile[chunks - len(cols) + s, at, :] + c for s, c in enumerate(cols)]
                    before = top_ref[at, :]
                    top = jnp.maximum(before, tree(vs, jnp.maximum))
                    total = tree([jnp.exp2(v - top) for v in vs] + [sum_ref[at, :] * jnp.exp2(before - top)], add)
                tops.append(top)
                sums.append(total)
            top = jnp.concatenate(tops, axis=0).T
            total = jnp.concatenate(sums, axis=0).T
            best = jnp.max(top, axis=0, keepdims=True)
            total = jnp.sum(total * jnp.exp2(top - best), axis=0, keepdims=True)
            part, line = k // (blocks // 2), k % (blocks // 2)
            hmine[i, part, line : line + 1, :] = best + jnp.log2(total)
            if line == blocks // 2 - 1:
                for s, (dev, _) in enumerate(peers):
                    send(hmine.at[i, part], hslots.at[i, part, s], hsem.at[i, part], hrsem.at[i, part], dev)

    def post(i, peers):
        for s, (dev, _) in enumerate(peers):
            send(mine.at[i], slots.at[i, s], ssem.at[i], rsem.at[i], dev)

    def arrive(i, peers):
        n = len(peers)
        wait_bytes(slots.at[i, pl.ds(0, n)], rsem.at[i])
        return [mine[i]] + [slots[i, s] for s in range(n)]

    def tree(parts, op):
        while len(parts) > 1:
            parts = [op(parts[t], parts[t + 1]) if t + 1 < len(parts) else parts[t] for t in range(0, len(parts), 2)]
        return parts[0]

    def add(u, v):
        return u + v

    def half_end(i, part, peers):
        n = len(peers)
        wait_bytes(hslots.at[i, part, pl.ds(0, n)], hrsem.at[i, part])
        parts = [hmine[i, part]] + [hslots[i, part, s] for s in range(n)]
        top = tree(parts, jnp.maximum)
        return lines(-(top + jnp.log2(tree([jnp.exp2(p - top) for p in parts], add))))

    def lines(vector):
        return [vector[s : s + 1, :] for s in range(vector.shape[0])]

    build(c_ref, x_ref, sq_i, y_ref, sq_j)
    lse_finish(LR1, c_ref, None, peers_a)
    build(ct_ref, y_ref, sq_j, x_ref, sq_i)
    for i, tile, here, there in (
        (LC1, ct_ref, peers_a, peers_b),
        (LR2, c_ref, peers_b, peers_a),
        (LC2, ct_ref, peers_a, peers_b),
    ):
        one = half_end(i - 1, 0, here)
        lse_start(tile, one)
        two = half_end(i - 1, 1, here)
        lse_finish(i, tile, two, there)
    for k, line in enumerate(one + two):
        fe_ref[lanes(k), :] = upright(line)

    for part in range(2):
        cols = half_end(LC2, part, peers_b)
        at_col = part * len(cols)
        for k in range(ki):
            totals = []
            for at in steps(k):
                up = fe_ref[at, :]
                parts = []
                for s, c in enumerate(cols):
                    e = jnp.exp2((up + c) + c_ref[at_col + s, at, :]).astype(BF16)
                    p_ref[at, lanes(at_col + s)] = e
                    parts.append(e.astype(F32))
                if part:
                    totals.append(tree(parts + [sum_ref[at, :]], add))
                else:
                    sum_ref[at, :] = tree(parts, add)
            if part:
                mine[MASS, k : k + 1, :] = jnp.sum(jnp.concatenate(totals, axis=0).T, axis=0, keepdims=True)
    post(MASS, peers_a)

    def wide_dot(left):
        return jnp.dot(left, p_ref[...], preferred_element_type=F32)

    def tall_dot(left):
        return jnp.dot(left, pt_ref[...], preferred_element_type=F32)

    xp_ref[...] = wide_dot(x_ref[...])
    for s in range(kj):
        mine[CMASS, s : s + 1, :] = xp_ref[feats : feats + 1, lanes(s)]
    post(CMASS, peers_b)
    for k in range(ki):
        for s in range(kj):
            pt_ref[lanes(s), lanes(k)] = p_ref[lanes(k), lanes(s)].T
    wait_bytes(gsl_a.at[pl.ds(0, na - 1)], gsem.at[7])
    wait_bytes(gsl_b.at[pl.ds(0, nb - 1)], gsem.at[5])
    for k in range(ki):
        row_ref[k : k + 1, :] = jnp.where(first1, gsl_a[2 * k], gsl_a[2 * k + 1])
    grad_f = row_ref[0:ki, :]
    for k in range(kj):
        row_ref[k : k + 1, :] = jnp.where(first1, gsl_b[2 * k], gsl_b[2 * k + 1])
    grad_g = row_ref[0:kj, :]

    def load_lhs(vector, width):
        high = vector.astype(BF16).astype(F32)
        rest = vector - high
        mid = rest.astype(BF16).astype(F32)
        low = rest - mid
        for s in range(width // LANES):
            lhs_ref[0:1, lanes(s)] = high[s : s + 1, :]
            lhs_ref[1:2, lanes(s)] = mid[s : s + 1, :]
            lhs_ref[2:3, lanes(s)] = low[s : s + 1, :]
        return lhs_ref[:, 0:width].astype(BF16)

    def keep(i, got):
        got = got[0:1] + got[1:2] + got[2:3]
        for s in range(got.shape[1] // LANES):
            mine[i, s : s + 1, :] = got[:, lanes(s)]

    def col_dot(i, vector):
        keep(i, wide_dot(load_lhs(vector, ti)))
        post(i, peers_b)

    row_mass = tree(arrive(MASS, peers_a), add)
    col_dot(PULL, grad_f / row_mass)
    yp_ref[...] = tall_dot(y_ref[...])
    col_mass = tree(arrive(CMASS, peers_b), add)
    residual = grad_g - tree(arrive(PULL, peers_b), add)

    def line_sum(v):
        return jnp.sum(v, axis=0, keepdims=True)

    def extra_post(i, peers):
        for s, (dev, _) in enumerate(peers):
            send(emine.at[i], eslots.at[i, s], essem.at[i], ersem.at[i], dev)

    def extra_arrive(i, peers):
        n = len(peers)
        wait_bytes(eslots.at[i, pl.ds(0, n)], ersem.at[i])
        got = tree([emine[i]] + [eslots[i, s] for s in range(n)], add)
        return jnp.sum(got, axis=1, keepdims=True)

    def spread(points, pulled, part, k):
        grad = 2.0 * (points.astype(F32) * pulled[feats : feats + 1, :] - pulled[0:feats, :])
        low, high = grad[0:half], grad[half:feats]
        part[2 * k] = jnp.where(first, low, pltpu.roll(high, pts, 1)).astype(BF16)
        part[2 * k + 1] = jnp.where(first, pltpu.roll(low, pts, 1), high).astype(BF16)

    def split(out, points, factors):
        rows = points.shape[0]
        for s, factor in enumerate(factors):
            v = points[:, lanes(s)].astype(F32) * factor
            high = v.astype(BF16)
            out[0:rows, lanes(s)] = high
            out[rows : 2 * rows, lanes(s)] = (v - high.astype(F32)).astype(BF16)

    rows = feats + 16

    def tgt_parts(g, us, ws, between):
        split(xu_ref, x_ref, us)
        got = wide_dot(xu_ref[...])
        between()
        for k in range(kj):
            pulled = got[0:rows, lanes(k)] + got[rows:, lanes(k)] + ws[k] * xp_ref[:, lanes(k)]
            spread(y_ref[0:feats, lanes(k)], pulled, part_b.at[g], k)
        for s, (dev, peer) in enumerate(peers_b):
            send(part_b.at[g, peer], rs_b.at[g, s], sgb.at[g], rgb.at[g], dev)

    def src_parts(g, us, pulled_of):
        for k in range(ki):
            spread(x_ref[0:feats, lanes(k)], pulled_of(k) + us[k] * yp_ref[:, lanes(k)], part_a.at[g], k)
        for s, (dev, peer) in enumerate(peers_a):
            send(part_a.at[g, peer], rs_a.at[g, s], sga.at[g], rga.at[g], dev)

    def early_gradients(on_row, on_col, residual, direction):
        us, ws = lines(on_row), lines(on_col)
        for t, vector in enumerate((on_col, residual, direction)):
            split(yw_ref.at[pl.ds(2 * rows * t, 2 * rows)], y_ref, lines(vector))
        got = tall_dot(yw_ref[...])
        for t in range(1, 3):
            at = 2 * rows * t
            yk_ref[t - 1] = got[at : at + rows] + got[at + rows : at + 2 * rows]

        def between():
            src_parts(0, us, lambda k: got[0:rows, lanes(k)] + got[rows : 2 * rows, lanes(k)])

        tgt_parts(0, us, ws, between)

    def late_gradients(on_row, on_col, beta):
        us, ws = lines(on_row), lines(on_col)

        def between():
            src_parts(1, us, lambda k: yk_ref[0, :, lanes(k)] + beta * yk_ref[1, :, lanes(k)])

        tgt_parts(1, us, ws, between)

    def joint_post(r, got, peers):
        got = got[0:1] + got[1:2] + got[2:3]
        for s in range(got.shape[1] // LANES):
            cmine[r, s // 4, s % 4 : s % 4 + 1, :] = got[:, lanes(s)]
        for s, (dev, _) in enumerate(peers):
            send(cmine.at[r], cslots.at[r, s], csem.at[r], crsem.at[r], dev)

    def joint_arrive(r, peers):
        n = len(peers)
        wait_bytes(cslots.at[r, pl.ds(0, n)], crsem.at[r])
        got = tree([cmine[r]] + [cslots[r, s] for s in range(n)], add)
        groups = got.shape[0] - 1
        return jnp.concatenate([got[t] for t in range(groups)], axis=0), jnp.sum(got[groups], axis=1, keepdims=True)

    dual = pulled_dual = direction = applied = norm = d_c_d = None
    tail = cmine.shape[1] - 1
    for it in range(CG):
        r_a, r_b = 2 * it, 2 * it + 1
        weighted = col_mass * residual
        cmine[r_a, tail, 0:1, :] = line_sum(residual * residual)
        cmine[r_a, tail, 1:2, :] = line_sum(weighted * residual)
        if it:
            cmine[r_a, tail, 2:3, :] = line_sum(weighted * direction)
        joint_post(r_a, tall_dot(load_lhs(residual, tj)), peers_a)
        if it == CG - 1:
            early_gradients((grad_f - pulled_dual) / row_mass, dual, residual, direction)
        fresh, scal = joint_arrive(r_a, peers_a)
        if it:
            beta = scal[0:1] / norm
            direction = residual + beta * direction
            applied = fresh + beta * applied
            d_c_d = scal[1:2] + 2.0 * beta * scal[2:3] + beta * beta * d_c_d
        else:
            direction, applied, d_c_d = residual, fresh, scal[1:2]
        norm = scal[0:1]
        back = applied / row_mass
        q_line = line_sum(applied * back)
        if it == CG - 1:
            emine[0, 0:1, :] = q_line
            extra_post(0, peers_b)
            late_gradients(-back, direction, beta)
            q_q = extra_arrive(0, peers_b)[0:1]
            alpha = norm / ((1.0 + TAU) * d_c_d - q_q)
            continue
        cmine[r_b, tail, 0:1, :] = q_line
        joint_post(r_b, wide_dot(load_lhs(back, ti)), peers_b)
        pulled, scal = joint_arrive(r_b, peers_b)
        alpha = norm / ((1.0 + TAU) * d_c_d - scal[0:1])
        dual = alpha * direction if it == 0 else dual + alpha * direction
        pulled_dual = alpha * applied if it == 0 else pulled_dual + alpha * applied
        image = (1.0 + TAU) * col_mass * direction - pulled
        residual = residual - alpha * image

    def collect(g, part, me, slot, n, sem):
        wait_bytes(slot.at[g], sem.at[g])
        return tree([part[g, me].astype(F32)] + [slot[g, s].astype(F32) for s in range(n)], add)

    def store(out, got):
        out[0:half, :] = got[:, 0:pts]
        out[half:feats, :] = got[:, pts:]

    base_a = collect(0, part_a, me_a, rs_a, na - 1, rga)
    base_b = collect(0, part_b, me_b, rs_b, nb - 1, rgb)
    store(osrc_ref, base_a + alpha * collect(1, part_a, me_a, rs_a, na - 1, rga))
    store(otgt_ref, base_b + alpha * collect(1, part_b, me_b, rs_b, nb - 1, rgb))

    wait_bytes(gath_b.at[pl.ds(0, nb - 1)], gsem.at[0])
    wait_bytes(gath_a.at[pl.ds(0, na - 1)], gsem.at[2])
    wait_bytes(gsl_b.at[pl.ds(0, nb - 1)], gsem.at[4])
    wait_bytes(gsl_a.at[pl.ds(0, na - 1)], gsem.at[6])
    for g in range(2):
        wait_bytes(rs_a.at[g], sga.at[g])
        wait_bytes(rs_b.at[g], sgb.at[g])
    over_a = (LR1, LR2, MASS)
    for i in range(MASS):
        for part in range(2):
            wait_bytes(hslots.at[i, part, pl.ds(0, len(peers_a if i in over_a else peers_b))], hsem.at[i, part])
    for i in range(MASS, ROUNDS):
        wait_bytes(slots.at[i, pl.ds(0, len(peers_a if i in over_a else peers_b))], ssem.at[i])
    for r in range(2 * CG - 1):
        wait_bytes(cslots.at[r, pl.ds(0, len(peers_a if r % 2 == 0 else peers_b))], csem.at[r])
    wait_bytes(eslots.at[0, pl.ds(0, len(peers_b))], essem.at[0])


def hand_over(one_ref, two_ref, first_ref, second_ref):
    first_ref[...] = one_ref[...]
    second_ref[...] = two_ref[...]


def body(sizes, src_points, tgt_points, grad_f, grad_g):
    nx, ny, nz, nc = sizes
    feats, pts = src_points.shape
    na, nb = nx * ny, nz * nc
    ti, tj = na * pts, nb * pts
    ki, kj = ti // LANES, tj // LANES
    n = max(na, nb) - 1
    k = max(ki, kj)
    half = feats // 2
    rows = feats + 16
    vmem = pl.BlockSpec(memory_space=pltpu.VMEM)
    out = jax.ShapeDtypeStruct((feats, pts), F32)
    both = pl.pallas_call(
        functools.partial(kernel, sizes),
        out_shape=(out, out),
        in_specs=[pl.BlockSpec(memory_space=pl.ANY)] * 4,
        out_specs=(vmem, vmem),
        scratch_shapes=[
            pltpu.VMEM((feats, pts), BF16),
            pltpu.VMEM((feats, pts), BF16),
            pltpu.VMEM((grad_f.shape[0] // LANES, LANES), F32),
            pltpu.VMEM((grad_g.shape[0] // LANES, LANES), F32),
            pltpu.VMEM((half, LANES), BF16),
            pltpu.VMEM((half, LANES), BF16),
            pltpu.VMEM((na, half, LANES), BF16),
            pltpu.VMEM((nb, half, LANES), BF16),
            pltpu.VMEM((1, LANES), F32),
            pltpu.VMEM((1, LANES), F32),
            pltpu.VMEM((na, 1, LANES), F32),
            pltpu.VMEM((nb, 1, LANES), F32),
            pltpu.VMEM((rows, ti), BF16),
            pltpu.VMEM((rows, tj), BF16),
            pltpu.VMEM((kj, ti, LANES), F32),
            pltpu.VMEM((ki, tj, LANES), F32),
            pltpu.VMEM((ti, tj), BF16),
            pltpu.VMEM((tj, ti), BF16),
            pltpu.VMEM((ti, LANES), F32),
            pltpu.VMEM((8, max(ti, tj)), F32),
            pltpu.VMEM((k, LANES), F32),
            pltpu.VMEM((2 * rows, ti), BF16),
            pltpu.VMEM((6 * rows, tj), BF16),
            pltpu.VMEM((rows, tj), F32),
            pltpu.VMEM((rows, ti), F32),
            pltpu.VMEM((2, rows, ti), F32),
            pltpu.VMEM((ROUNDS, k, LANES), F32),
            pltpu.VMEM((ROUNDS, n, k, LANES), F32),
            pltpu.VMEM((4, 2, k // 2, LANES), F32),
            pltpu.VMEM((4, 2, n, k // 2, LANES), F32),
            pltpu.VMEM((max(ti, tj), LANES), F32),
            pltpu.VMEM((max(ti, tj), LANES), F32),
            pltpu.VMEM((2 * CG - 1, k // 4 + 1, 4, LANES), F32),
            pltpu.VMEM((2 * CG - 1, n, k // 4 + 1, 4, LANES), F32),
            pltpu.VMEM((1, 4, LANES), F32),
            pltpu.VMEM((1, n, 4, LANES), F32),
            pltpu.VMEM((2, na, half, LANES), BF16),
            pltpu.VMEM((2, nb, half, LANES), BF16),
            pltpu.VMEM((2, na - 1, half, LANES), BF16),
            pltpu.VMEM((2, nb - 1, half, LANES), BF16),
            pltpu.SemaphoreType.DMA((4,)),
            pltpu.SemaphoreType.DMA((8,)),
            pltpu.SemaphoreType.DMA((4, 2)),
            pltpu.SemaphoreType.DMA((4, 2)),
            pltpu.SemaphoreType.DMA((2 * CG - 1,)),
            pltpu.SemaphoreType.DMA((2 * CG - 1,)),
            pltpu.SemaphoreType.DMA((ROUNDS,)),
            pltpu.SemaphoreType.DMA((ROUNDS,)),
            pltpu.SemaphoreType.DMA((1,)),
            pltpu.SemaphoreType.DMA((1,)),
            pltpu.SemaphoreType.DMA((2,)),
            pltpu.SemaphoreType.DMA((2,)),
            pltpu.SemaphoreType.DMA((2,)),
            pltpu.SemaphoreType.DMA((2,)),
        ],
        compiler_params=pltpu.CompilerParams(
            collective_id=0, has_side_effects=True, vmem_limit_bytes=56 * 1024 * 1024
        ),
        name="transport",
    )(src_points, tgt_points, grad_f.reshape(-1, LANES), grad_g.reshape(-1, LANES))
    return pl.pallas_call(
        hand_over, out_shape=(out, out), in_specs=[vmem] * 2, out_specs=(vmem, vmem), name="hand_over"
    )(*both)


def solution(mesh):
    rows, cols = mesh.shape["row"], mesh.shape["col"]
    sizes = (4, cols // 4, rows // 2, 2)
    in_specs = (P(None, ("row", "col")), P(None, ("col", "row")), P("row"), P("col"))
    out_specs = (P(None, ("row", "col")), P(None, ("col", "row")))
    return jax.shard_map(
        functools.partial(body, sizes), mesh=mesh, in_specs=in_specs, out_specs=out_specs, check_vma=False
    )
```
